32 devices in a mesh: mode: 16 (over z, x, core), rank: 2 (over y).
Axes of the slice: x: 2, y: 2, z: 4, core: 2. Of those that a mesh axis runs over, the one named last changes fastest.
Arguments:
- start_core: float32 [256, 128, 128], P('mode', 'rank'), may hold values from -108 to 108
- right_side: float32 [256, 128, 128], P('mode', 'rank'), may hold values from -108 to 108
- left_interface: float32 [3, 128, 128], replicated, may hold values from -1 to 2
- right_interface: float32 [3, 128, 128], replicated, may hold values from -1 to 2
- couplings: float32 [3, 3, 3, 256], P(None, None, None, 'mode'), may hold values from -5 to 5
Outputs:
- orthonormal_core: float32 [256, 128, 128], P('mode', 'rank')
- triangle: float32 [128, 128], replicated
- next_interface: float32 [3, 128, 128], P(None, 'rank')
The draws below stay inside these ranges and needn't reach their ends.
All inputs are finite; a program needn't handle non-finite values.
Results may differ from the reference program's by a relative error of at most 0.00027.
Values sent between devices are 32-bit elements; how exact they have to be, the bound alone decides.
A program may use at most 64 MiB of HBM per device.

```python
import math
import jax
import jax.numpy as jnp
from jax import lax

R = 128
OPR = 3
MODE = 256


def draw_field(key):
    first, second = jax.random.split(key)
    ramp = 1.0 + 2.0 * jnp.arange(MODE, dtype=jnp.float32) / max(MODE - 1, 1)
    scales = jnp.exp(jax.random.uniform(second, (R,), minval=math.log(0.3), maxval=math.log(3.0)))
    values = jax.random.truncated_normal(first, -4.0, 4.0, (MODE, R, R))
    return (values * ramp[:, None, None] * scales[None, None, :]).astype(jnp.float32)


def draw_start_core(key, part):
    return draw_field(jax.random.fold_in(key, 11))


def draw_right_side(key, part):
    return draw_field(jax.random.fold_in(key, 23))


def draw_interface(key):
    values = jax.random.truncated_normal(key, -4.0, 4.0, (OPR, R, R)) / math.sqrt(R)
    first_slice = (jnp.arange(OPR) == 0)[:, None, None]
    identity = jnp.eye(R, dtype=jnp.float32)[None, :, :]
    return jnp.where(first_slice, 0.5 * values + identity, values).astype(jnp.float32)


def draw_left_interface(key, part):
    return draw_interface(jax.random.fold_in(key, 37))


def draw_right_interface(key, part):
    return draw_interface(jax.random.fold_in(key, 41))


def draw_couplings(key, part):
    first, second = jax.random.split(jax.random.fold_in(key, 53))
    raw = jax.random.truncated_normal(first, -4.0, 4.0, (OPR, OPR, 3, MODE))
    base = 0.2 * raw
    centre = jax.random.uniform(second, (MODE,), minval=1.0, maxval=2.0)
    outer = jnp.arange(OPR)[:, None, None, None]
    inner = jnp.arange(OPR)[None, :, None, None]
    offset = jnp.arange(3)[None, None, :, None]
    leading = (outer == 0) & (inner == 0)
    chosen = leading & (offset == 1)
    sides = leading & (offset != 1)
    values = jnp.where(sides, 1.2 * raw, base)
    return jnp.where(chosen, centre[None, None, None, :], values).astype(jnp.float32)


def setup_inputs(seed: int = 0) -> dict:
    key_list = jax.random.split(jax.random.key(seed), 6)
    start_core = draw_start_core(jax.random.fold_in(key_list[5], 71), 0)
    right_side = draw_right_side(jax.random.fold_in(key_list[5], 71), 0)
    left_interface = draw_left_interface(jax.random.fold_in(key_list[5], 71), 0)
    right_interface = draw_right_interface(jax.random.fold_in(key_list[5], 71), 0)
    couplings = draw_couplings(jax.random.fold_in(key_list[5], 71), 0)
    return dict(start_core=start_core, right_side=right_side, left_interface=left_interface, right_interface=right_interface, couplings=couplings)


highest = lax.Precision.HIGHEST

def banded(field, couplings, form):
    length = field.shape[1]
    padded = jnp.pad(field, ((0, 0), (1, 1), (0, 0), (0, 0)))
    total = jnp.einsum(form, couplings[:, :, 0, :], padded[:, 0:length], precision=highest)
    for offset in range(1, 3):
        total = total + jnp.einsum(form, couplings[:, :, offset, :], padded[:, offset:offset + length], precision=highest)
    return total

def apply_operator(field, left_interface, right_interface, couplings):
    contracted = jnp.einsum('ybc,icd->yibd', right_interface, field, precision=highest)
    coupled = banded(contracted, couplings, 'xyi,yibd->xibd')
    return jnp.einsum('xad,xibd->iba', left_interface, coupled, precision=highest)

def reference(start_core, right_side, left_interface, right_interface, couplings):
    scale = 1.0 / (R * MODE)
    applied = apply_operator(start_core, left_interface, right_interface, couplings)
    residual = right_side - applied
    image = apply_operator(residual, left_interface, right_interface, couplings)
    alpha = jnp.sum(residual * image) / jnp.sum(image * image)
    core = start_core + alpha * residual
    gram = jnp.einsum('ica,ida->cd', core, core, precision=highest) * scale
    lower = jnp.linalg.cholesky(gram)
    inverse = jax.scipy.linalg.solve_triangular(lower, jnp.eye(R, dtype=jnp.float32), lower=True)
    basis = jnp.einsum('bc,ica->iba', inverse, core, precision=highest)
    mixed = jnp.einsum('xad,ibd->xiba', left_interface, basis, precision=highest)
    moved = banded(mixed, couplings, 'xyi,xiba->yiba')
    interface = jnp.einsum('ipa,yiqa->yqp', basis, moved, precision=highest) * scale
    return (basis, lower.T, interface)
```

```python
import functools

import jax
import jax.numpy as jnp
from jax import lax
from jax.experimental import pallas as pl
from jax.experimental.pallas import tpu as pltpu
from jax.sharding import PartitionSpec as P

HIGH = lax.Precision.HIGH
HIGHEST = lax.Precision.HIGHEST
F32 = jnp.float32


def dot(a, b, dims=((1,), (0,)), precision=HIGH):
    return lax.dot_general(a, b, (dims, ((), ())), precision=precision, preferred_element_type=F32)


def contract_right(source, weights, target, count, width):
    def body(p, carry):
        pair = jnp.concatenate([source[2 * p], source[2 * p + 1]], axis=1)
        out = dot(weights[...], pair)
        for k in range(3):
            rows = out[k * width : (k + 1) * width]
            target[k, 2 * p] = rows[:, :width]
            target[k, 2 * p + 1] = rows[:, width:]
        return carry

    lax.fori_loop(0, count // 2, body, 0)


def coupled(field, factors, row, index, inner_first, width):
    step = min(64, width)
    pieces = []
    for start in range(0, width, step):
        sums = [None] * 3
        for k in range(3):
            for s in range(3):
                block = field[k, index + s, start : start + step, :]
                for o in range(3):
                    pair = (k * 3 + o) if inner_first else (o * 3 + k)
                    term = factors[row, pl.ds(pair * 3 + s, 1), :] * block
                    sums[o] = term if sums[o] is None else sums[o] + term
        pieces.append(sums)
    return [jnp.concatenate([piece[o] for piece in pieces], axis=0) for o in range(3)]


def eliminate(work, width):
    size = 8
    sub = lax.broadcasted_iota(jnp.int32, (size, 2 * width), 0)
    for k in range(width // size):
        base = k * size
        panel = work[base : base + size, :]
        rows = [jnp.broadcast_to(panel[i : i + 1, :], (size, 2 * width)) for i in range(size)]
        entry = {}
        for j in range(size):
            column = jnp.broadcast_to(panel[:, base + j : base + j + 1], (size, width))
            for i in range(j, size):
                entry[i, j] = jnp.broadcast_to(column[i : i + 1, :], (size, width))
        for j in range(size):
            pivot = entry[j, j]
            inv = lax.rsqrt(pivot)
            inv = inv * (1.5 - 0.5 * (pivot * inv) * inv)
            rows[j] = rows[j] * jnp.concatenate([inv, inv], axis=1)
            scaled = {i: entry[i, j] * inv for i in range(j + 1, size)}
            for c in range(j + 1, size):
                for i in range(c, size):
                    entry[i, c] = entry[i, c] - scaled[i] * scaled[c]
            for i in range(j + 1, size):
                factor = jnp.concatenate([scaled[i], scaled[i]], axis=1)
                rows[i] = rows[i] - factor * rows[j]
        done = rows[0]
        for i in range(1, size):
            done = jnp.where(sub == i, rows[i], done)
        work[base : base + size, :] = done
        if base + size < width:
            update = dot(done[:, :width], done, ((0,), (0,)), HIGHEST)
            work[base + size :, :] = work[base + size :, :] - update[base + size :, :]


def kernel(
    nm, nr, ml, scale,
    x_ref, f_ref, l_ref, p_ref, c_ref,
    q_out, tri_out, n_out,
    xf, ff, ce, tt, res, qb, lt_rows, lt_cols, work,
    gpart, grecv, gsend, gbrecv, gfull,
    ssend, srecv, sbsend, sbrecv,
    npart, nrecv, nsend, nbrecv, nfull,
    x_send, x_recv, xe_send, xe_recv,
    f_send, f_recv, fe_send, fe_recv,
    ce_send, ce_recv,
    ga_send, ga_recv, gb_send, gb_recv, gc_send, gc_recv,
    sa_send, sa_recv, sb_send, sb_recv,
    na_send, na_recv, nb_send, nb_recv, nc_send, nc_recv,
    q_send, q_recv,
):
    height, piece, width = x_ref.shape
    mine = height // nr
    mh = nm // ml
    na = nr * ml
    m = lax.axis_index("mode")
    r = lax.axis_index("rank")
    low = lax.rem(m, ml)
    high = lax.div(m, ml)
    g = r * ml + low
    has_prev = m > 0
    has_next = m < nm - 1

    def at_a(t):
        return {"mode": high * ml + lax.rem(t, ml), "rank": lax.div(t, ml)}

    def at_b(t):
        return {"mode": t * ml + low, "rank": r}

    def at_r(t):
        return {"mode": m, "rank": t}

    def remote(src, dst, send, recv, where):
        return pltpu.make_async_remote_copy(
            src_ref=src, dst_ref=dst, send_sem=send, recv_sem=recv,
            device_id=where, device_id_type=pl.DeviceIdType.MESH,
        )

    def greet(where):
        pl.semaphore_signal(
            barrier, inc=1, device_id=where, device_id_type=pl.DeviceIdType.MESH
        )

    barrier = pltpu.get_barrier_semaphore()
    for d in range(1, na):
        greet(at_a(lax.rem(g + d, na)))
    for d in range(1, mh):
        greet(at_b(lax.rem(high + d, mh)))

    @pl.when(has_prev)
    def _():
        for t in range(nr):
            greet({"mode": m - 1, "rank": t})

    @pl.when(has_next)
    def _():
        for t in range(nr):
            greet({"mode": m + 1, "rank": t})

    pl.semaphore_wait(
        barrier, na - 1 + mh - 1 + nr * (has_prev.astype(jnp.int32) + has_next.astype(jnp.int32))
    )

    columns = pl.ds(pl.multiple_of(r * piece, piece), piece)

    def span(t, halo):
        first = max(0, mine * t - halo)
        last = min(height, mine * t + mine + halo)
        return first, last - first, first - (mine * t - halo)

    moves = []
    for source, target, halo, send, recv, esend, erecv in (
        (x_ref, xf, 2, x_send, x_recv, xe_send, xe_recv),
        (f_ref, ff, 1, f_send, f_recv, fe_send, fe_recv),
    ):
        up = remote(
            source.at[pl.ds(height - halo, halo)], target.at[pl.ds(0, halo), columns],
            esend.at[0], erecv.at[r], {"mode": m + 1, "rank": 0},
        )
        down = remote(
            source.at[pl.ds(0, halo)], target.at[pl.ds(mine + halo, halo), columns],
            esend.at[1], erecv.at[r], {"mode": m - 1, "rank": nr - 1},
        )
        pl.when(has_next)(up.start)
        pl.when(has_prev)(down.start)
        across = []
        for t in range(nr):
            first, count, offset = span(t, halo)
            copy = remote(
                source.at[pl.ds(first, count)], target.at[pl.ds(offset, count), columns],
                send.at[t], recv.at[r], at_r(t),
            )
            pl.when(r != t)(copy.start)
            across.append(copy)
        moves.append((up, down, across))
        if source is x_ref:
            c_up = remote(
                c_ref.at[pl.ds(height - 1, 1)], ce.at[pl.ds(0, 1)],
                ce_send.at[0], ce_recv.at[0], {"mode": m + 1, "rank": r},
            )
            c_down = remote(
                c_ref.at[pl.ds(0, 1)], ce.at[pl.ds(mine + 1, 1)],
                ce_send.at[1], ce_recv.at[1], {"mode": m - 1, "rank": r},
            )
            pl.when((r == 0) & has_next)(c_up.start)
            pl.when((r == nr - 1) & has_prev)(c_down.start)

    for t in range(nr):

        @pl.when(r == t)
        def _():
            for source, target, halo in ((x_ref, xf, 2), (f_ref, ff, 1)):
                first, count, offset = span(t, halo)
                target[offset : offset + count, t * piece : (t + 1) * piece, :] = source[
                    first : first + count
                ]
            first, count, offset = span(t, 1)
            ce[offset : offset + count] = c_ref[first : first + count]

    @pl.when((r == 0) & jnp.logical_not(has_prev))
    def _():
        xf[0:2] = jnp.zeros((2, width, width), F32)
        ff[0:1] = jnp.zeros((1, width, width), F32)
        ce[0:1] = jnp.zeros((1,) + ce.shape[1:], F32)

    @pl.when((r == nr - 1) & jnp.logical_not(has_next))
    def _():
        xf[mine + 2 :] = jnp.zeros((2, width, width), F32)
        ff[mine + 1 :] = jnp.zeros((1, width, width), F32)
        ce[mine + 1 :] = jnp.zeros((1,) + ce.shape[1:], F32)

    for k in range(3):
        turned = l_ref[k].T
        lt_rows[k * width : (k + 1) * width, :] = turned
        lt_cols[:, k * width : (k + 1) * width] = turned

    low_edge = (r == 0) & has_prev
    high_edge = (r == nr - 1) & has_next

    def arrive(target, halo, recv, erecv, send, esend):
        for t in range(nr):
            part = pl.ds(t * piece, piece)
            for mine_rank in range(nr):
                if mine_rank == t:
                    continue
                _, count, offset = span(mine_rank, halo)
                block = target.at[pl.ds(offset, count), part]
                pl.when(r == mine_rank)(
                    remote(block, block, send.at[t], recv.at[t], at_r(t)).wait_recv
                )
            block = target.at[pl.ds(0, halo), part]
            pl.when(low_edge)(remote(block, block, esend.at[0], erecv.at[t], at_r(t)).wait_recv)
            block = target.at[pl.ds(mine + halo, halo), part]
            pl.when(high_edge)(remote(block, block, esend.at[1], erecv.at[t], at_r(t)).wait_recv)

    arrive(xf, 2, x_recv, xe_recv, x_send, xe_send)
    pl.when(low_edge)(c_up.wait_recv)
    pl.when(high_edge)(c_down.wait_recv)

    contract_right(xf, p_ref, tt, mine + 4, width)
    arrive(ff, 1, f_recv, fe_recv, f_send, fe_send)

    def applied(index, row):
        parts = coupled(tt, ce, row, index, False, width)
        return dot(jnp.concatenate(parts, axis=1), lt_rows[...])

    def residual_body(i, carry):
        res[i] = ff[i] - applied(i, i)
        return carry

    lax.fori_loop(0, mine + 2, residual_body, 0)

    def gram_body(i, total):
        both = jnp.concatenate([xf[i + 2], res[i + 1]], axis=0)
        return total + dot(both, both, ((1,), (1,)))

    total = lax.fori_loop(0, mine, gram_body, jnp.zeros((2 * width, 2 * width), F32))
    cross = total[:width, width:]
    pieces = jnp.concatenate(
        [total[:width, :width], cross + cross.T, total[width:, width:]], axis=0
    )
    gpart[...] = pieces.reshape(gpart.shape)

    def scatter(part, recv_buf, send, recv):
        for d in range(1, na):
            t = lax.rem(g + d, na)
            remote(part.at[t], recv_buf.at[g], send.at[d - 1], recv.at[d - 1], at_a(t)).start()
        recv_buf[g] = part[g]

    def spread(part, recv_buf, send, recv):
        for d in range(1, na):
            t = lax.rem(g + d, na)
            remote(part, recv_buf.at[g], send.at[d - 1], recv.at[d - 1], at_a(t)).start()
        recv_buf[g] = part[...]

    def gathered(recv_buf, send, recv):
        for d in range(1, na):
            t = lax.rem(g + na - d, na)
            block = recv_buf.at[t]
            remote(block, block, send.at[d - 1], recv.at[d - 1], at_a(t)).wait_recv()

    def exchange_b(part, recv_buf, send, recv):
        for d in range(1, mh):
            t = lax.rem(high + d, mh)
            remote(part, recv_buf.at[high], send.at[d - 1], recv.at[d - 1], at_b(t)).start()
        recv_buf[high] = part[...]

    def gathered_b(recv_buf, send, recv):
        for d in range(1, mh):
            t = lax.rem(high + mh - d, mh)
            block = recv_buf.at[t]
            remote(block, block, send.at[d - 1], recv.at[d - 1], at_b(t)).wait_recv()

    def add_up(recv_buf, count):
        out = recv_buf[0]
        for t in range(1, count):
            out = out + recv_buf[t]
        return out

    scatter(gpart, grecv, ga_send, ga_recv)
    contract_right(res, p_ref, tt, mine + 2, width)
    gathered(grecv, ga_send, ga_recv)
    gsend[...] = add_up(grecv, na)
    exchange_b(gsend, gbrecv, gb_send, gb_recv)

    def fold(values):
        return jnp.sum(values.reshape(width // 8, 8, width), axis=0)

    def image_body(i, carry):
        along, energy = carry
        image = applied(i, i + 1)
        return along + fold(res[i + 1] * image), energy + fold(image * image)

    zero = jnp.zeros((8, width), F32)
    along, energy = lax.fori_loop(0, mine, image_body, (zero, zero))
    ssend[0:1, :] = jnp.sum(along, axis=0, keepdims=True)
    ssend[1:2, :] = jnp.sum(energy, axis=0, keepdims=True)
    ssend[2:8, :] = jnp.zeros((6, width), F32)
    spread(ssend, srecv, sa_send, sa_recv)
    gathered_b(gbrecv, gb_send, gb_recv)
    gfull[g] = add_up(gbrecv, mh)
    for d in range(1, na):
        t = lax.rem(g + d, na)
        remote(gfull.at[g], gfull.at[g], gc_send.at[d - 1], gc_recv.at[d - 1], at_a(t)).start()
    gathered(srecv, sa_send, sa_recv)
    sbsend[...] = add_up(srecv, na)
    exchange_b(sbsend, sbrecv, sb_send, sb_recv)
    gathered(gfull, gc_send, gc_recv)
    gathered_b(sbrecv, sb_send, sb_recv)
    sums = jnp.sum(add_up(sbrecv, mh), axis=1, keepdims=True)
    alpha = sums[0:1, :] / sums[1:2, :]

    grams = gfull[...].reshape(3 * width, width)
    gram = (
        grams[:width] + alpha * grams[width : 2 * width] + (alpha * alpha) * grams[2 * width :]
    ) * scale
    rows = lax.broadcasted_iota(jnp.int32, (width, width), 0)
    lanes = lax.broadcasted_iota(jnp.int32, (width, width), 1)
    work[:, :width] = gram
    work[:, width:] = jnp.where(rows == lanes, 1.0, 0.0).astype(F32)
    eliminate(work, width)
    tri_out[...] = jnp.where(lanes >= rows, work[:, :width], 0.0)
    inverse = jnp.where(lanes <= rows, work[:, width:], 0.0)

    def basis_body(p, carry):
        pair = jnp.concatenate(
            [xf[2 * p + 1] + alpha * res[2 * p], xf[2 * p + 2] + alpha * res[2 * p + 1]], axis=1
        )
        out = dot(inverse, pair)
        qb[2 * p] = out[:, :width]
        qb[2 * p + 1] = out[:, width:]
        return carry

    lax.fori_loop(0, (mine + 2) // 2, basis_body, 0)
    slab = pl.ds(r * mine, mine)
    for d in range(1, nr):
        t = lax.rem(r + d, nr)
        remote(
            qb.at[pl.ds(1, mine), pl.ds(pl.multiple_of(t * piece, piece), piece)],
            q_out.at[slab], q_send.at[d - 1], q_recv.at[d - 1], at_r(t),
        ).start()

    def mixed_body(i, carry):
        out = dot(qb[i], lt_cols[...])
        for k in range(3):
            tt[k, i] = out[:, k * width : (k + 1) * width]
        return carry

    lax.fori_loop(0, mine + 2, mixed_body, 0)

    def interface_body(i, total):
        parts = coupled(tt, ce, i + 1, i, True, width)
        return total + dot(jnp.concatenate(parts, axis=0), qb[i + 1], ((1,), (1,)))

    total = lax.fori_loop(0, mine, interface_body, jnp.zeros((3 * width, width), F32)) * scale
    total = total.reshape(3, nr, piece, width)
    for t in range(nr):
        npart[t * ml : (t + 1) * ml] = total[:, t].reshape((ml,) + npart.shape[1:])
    scatter(npart, nrecv, na_send, na_recv)
    q_out[slab] = qb[1 : mine + 1, columns, :]
    gathered(nrecv, na_send, na_recv)
    nsend[...] = add_up(nrecv, na)
    exchange_b(nsend, nbrecv, nb_send, nb_recv)
    gathered_b(nbrecv, nb_send, nb_recv)
    nfull[low] = add_up(nbrecv, mh)

    def at_c(t):
        return {"mode": high * ml + t, "rank": r}

    for d in range(1, ml):
        t = lax.rem(low + d, ml)
        remote(
            nfull.at[low], nfull.at[low], nc_send.at[d - 1], nc_recv.at[d - 1], at_c(t)
        ).start()
    for d in range(1, ml):
        t = lax.rem(low + ml - d, ml)
        block = nfull.at[t]
        remote(block, block, nc_send.at[d - 1], nc_recv.at[d - 1], at_c(t)).wait_recv()
    n_out[...] = nfull[...]

    for d in range(1, nr):
        t = lax.rem(r + nr - d, nr)
        block = q_out.at[pl.ds(t * mine, mine)]
        remote(block, block, q_send.at[d - 1], q_recv.at[d - 1], at_r(t)).wait_recv()

    for up, down, across in moves:
        pl.when(has_next)(up.wait_send)
        pl.when(has_prev)(down.wait_send)
        for t in range(nr):
            pl.when(r != t)(across[t].wait_send)
    pl.when((r == 0) & has_next)(c_up.wait_send)
    pl.when((r == nr - 1) & has_prev)(c_down.wait_send)
    for send, block, count in (
        (ga_send, gpart.at[0], na), (gc_send, gfull.at[0], na), (sa_send, ssend, na),
        (na_send, npart.at[0], na), (gb_send, gsend, mh), (sb_send, sbsend, mh),
        (nb_send, nsend, mh), (nc_send, nfull.at[0], ml), (q_send, q_out.at[pl.ds(0, mine)], nr),
    ):
        for d in range(1, count):
            remote(block, block, send.at[d - 1], send.at[d - 1], at_r(r)).wait_send()


def shards(nm, nr, start_core, right_side, left_interface, right_interface, couplings):
    height, piece, width = start_core.shape
    mine = height // nr
    ml = max(1, min(nm, 8 // nr))
    mh = nm // ml
    na = nr * ml
    scale = 1.0 / (height * nm * width)
    flat = couplings.reshape(27, height).T
    spread = jnp.broadcast_to(
        jnp.pad(flat, ((0, 0), (0, 5)))[:, :, None], (height, 32, width)
    )
    grows = 3 * width // na
    nrows = 3 * piece // ml
    vmem = lambda *shape: pltpu.VMEM(shape, F32)
    sem = lambda count: pltpu.SemaphoreType.DMA((max(1, count),))
    scratch = [
        vmem(mine + 4, width, width), vmem(mine + 2, width, width), vmem(mine + 2, 32, width),
        vmem(3, mine + 4, width, width), vmem(mine + 2, width, width),
        vmem(mine + 2, width, width), vmem(3 * width, width), vmem(width, 3 * width),
        vmem(width, 2 * width),
        vmem(na, grows, width), vmem(na, grows, width), vmem(grows, width),
        vmem(mh, grows, width), vmem(na, grows, width),
        vmem(8, width), vmem(na, 8, width), vmem(8, width), vmem(mh, 8, width),
        vmem(na, nrows, width), vmem(na, nrows, width), vmem(nrows, width),
        vmem(mh, nrows, width), vmem(ml, nrows, width),
        sem(nr), sem(nr), sem(2), sem(nr),
        sem(nr), sem(nr), sem(2), sem(nr),
        sem(2), sem(2),
        sem(na), sem(na), sem(mh), sem(mh), sem(na), sem(na),
        sem(na), sem(na), sem(mh), sem(mh),
        sem(na), sem(na), sem(mh), sem(mh), sem(ml), sem(ml),
        sem(nr), sem(nr),
    ]
    space = pl.BlockSpec(memory_space=pltpu.VMEM)
    basis, triangle, interface = pl.pallas_call(
        functools.partial(kernel, nm, nr, ml, scale),
        out_shape=(
            jax.ShapeDtypeStruct((height, piece, width), F32),
            jax.ShapeDtypeStruct((width, width), F32),
            jax.ShapeDtypeStruct((ml, nrows, width), F32),
        ),
        in_specs=[space] * 5,
        out_specs=(space,) * 3,
        scratch_shapes=scratch,
        compiler_params=pltpu.CompilerParams(
            collective_id=0, has_side_effects=True, vmem_limit_bytes=40 * 1024 * 1024
        ),
    )(
        start_core, right_side, left_interface,
        right_interface.reshape(3 * width, width), spread,
    )
    return basis, triangle, interface.reshape(3, piece, width)


def solution(mesh):
    placed = (
        P("mode", "rank", None),
        P("mode", "rank", None),
        P(),
        P(),
        P(None, None, None, "mode"),
    )
    return jax.shard_map(
        functools.partial(shards, mesh.shape["mode"], mesh.shape["rank"]),
        mesh=mesh,
        in_specs=placed,
        out_specs=(P("mode", "rank", None), P(), P(None, "rank", None)),
        check_vma=False,
    )
```

```python
import functools

import jax
import jax.numpy as jnp
from jax import lax
from jax.experimental import pallas as pl
from jax.experimental.pallas import tpu as pltpu
from jax.sharding import PartitionSpec as P

HIGH = lax.Precision.HIGH
HIGHEST = lax.Precision.HIGHEST
F32 = jnp.float32


def dot(a, b, dims=((1,), (0,)), precision=HIGH):
    return lax.dot_general(a, b, (dims, ((), ())), precision=precision, preferred_element_type=F32)


def contract_right(source, weights, target, count, width):
    def body(p, carry):
        pair = jnp.concatenate([source[2 * p], source[2 * p + 1]], axis=1)
        out = dot(weights[...], pair)
        for k in range(3):
            rows = out[k * width : (k + 1) * width]
            target[k, 2 * p] = rows[:, :width]
            target[k, 2 * p + 1] = rows[:, width:]
        return carry

    lax.fori_loop(0, count // 2, body, 0)


def coupled(field, factors, row, index, inner_first, width):
    step = min(64, width)
    pieces = []
    for start in range(0, width, step):
        sums = [None] * 3
        for k in range(3):
            for s in range(3):
                block = field[k, index + s, start : start + step, :]
                for o in range(3):
                    pair = (k * 3 + o) if inner_first else (o * 3 + k)
                    term = factors[row, pl.ds(pair * 3 + s, 1), :] * block
                    sums[o] = term if sums[o] is None else sums[o] + term
        pieces.append(sums)
    return [jnp.concatenate([piece[o] for piece in pieces], axis=0) for o in range(3)]


def coupled_pair(field, factors, row, index, inner_first, width):
    return [coupled(field, factors, row + d, index + d, inner_first, width) for d in range(2)]


def eliminate(work, width):
    size = 8
    sub = lax.broadcasted_iota(jnp.int32, (size, 2 * width), 0)
    for k in range(width // size):
        base = k * size
        panel = work[base : base + size, :]
        rows = [jnp.broadcast_to(panel[i : i + 1, :], (size, 2 * width)) for i in range(size)]
        entry = {}
        for j in range(size):
            column = jnp.broadcast_to(panel[:, base + j : base + j + 1], (size, width))
            for i in range(j, size):
                entry[i, j] = jnp.broadcast_to(column[i : i + 1, :], (size, width))
        for j in range(size):
            pivot = entry[j, j]
            inv = lax.rsqrt(pivot)
            inv = inv * (1.5 - 0.5 * (pivot * inv) * inv)
            rows[j] = rows[j] * jnp.concatenate([inv, inv], axis=1)
            scaled = {i: entry[i, j] * inv for i in range(j + 1, size)}
            for c in range(j + 1, size):
                for i in range(c, size):
                    entry[i, c] = entry[i, c] - scaled[i] * scaled[c]
            for i in range(j + 1, size):
                factor = jnp.concatenate([scaled[i], scaled[i]], axis=1)
                rows[i] = rows[i] - factor * rows[j]
        done = rows[0]
        for i in range(1, size):
            done = jnp.where(sub == i, rows[i], done)
        work[base : base + size, :] = done
        if base + size < width:
            update = dot(done[:, :width], done, ((0,), (0,)), HIGHEST)
            work[base + size :, :] = work[base + size :, :] - update[base + size :, :]


def kernel(
    nm, nr, ml, scale,
    x_ref, f_ref, l_hbm, p_hbm, raw_ref,
    q_out, tri_out, n_out,
    l_ref, p_ref, c_ref, own_sem,
    xf, ff, ce, tt, res, qb, lt_rows, lt_cols, work,
    gpart, grecv, gsend, gbrecv, gfull,
    ssend, srecv, sbsend, sbrecv,
    npart, nrecv, nsend, nbrecv, nfull,
    x_send, x_recv, xe_send, xe_recv,
    f_send, f_recv, fe_send, fe_recv,
    ce_send, ce_recv,
    ga_send, ga_recv, gb_send, gb_recv, gc_send, gc_recv,
    sa_send, sa_recv, sb_send, sb_recv,
    na_send, na_recv, nb_send, nb_recv, nc_send, nc_recv,
    q_send, q_recv,
):
    height, piece, width = x_ref.shape
    mine = height // nr
    mh = nm // ml
    na = nr * ml
    m = lax.axis_index("mode")
    r = lax.axis_index("rank")
    low = lax.rem(m, ml)
    high = lax.div(m, ml)
    g = r * ml + low
    has_prev = m > 0
    has_next = m < nm - 1

    def at_a(t):
        return {"mode": high * ml + lax.rem(t, ml), "rank": lax.div(t, ml)}

    def at_b(t):
        return {"mode": t * ml + low, "rank": r}

    def at_r(t):
        return {"mode": m, "rank": t}

    def remote(src, dst, send, recv, where):
        return pltpu.make_async_remote_copy(
            src_ref=src, dst_ref=dst, send_sem=send, recv_sem=recv,
            device_id=where, device_id_type=pl.DeviceIdType.MESH,
        )

    def greet(where):
        pl.semaphore_signal(
            barrier, inc=1, device_id=where, device_id_type=pl.DeviceIdType.MESH
        )

    fetch_l = pltpu.make_async_copy(l_hbm, l_ref, own_sem.at[0])
    fetch_p = pltpu.make_async_copy(p_hbm, p_ref, own_sem.at[1])
    fetch_l.start()
    fetch_p.start()

    barrier = pltpu.get_barrier_semaphore()
    for d in range(1, na):
        greet(at_a(lax.rem(g + d, na)))
    for d in range(1, mh):
        greet(at_b(lax.rem(high + d, mh)))

    @pl.when(has_prev)
    def _():
        for t in range(nr):
            greet({"mode": m - 1, "rank": t})

    @pl.when(has_next)
    def _():
        for t in range(nr):
            greet({"mode": m + 1, "rank": t})

    for o in range(3):
        for k in range(3):
            block = raw_ref[o, k]
            first = (o * 3 + k) * 3
            for i in range(height):
                c_ref[i, first : first + 3, :] = jnp.broadcast_to(block[:, i : i + 1], (3, width))

    pl.semaphore_wait(
        barrier, na - 1 + mh - 1 + nr * (has_prev.astype(jnp.int32) + has_next.astype(jnp.int32))
    )

    columns = pl.ds(pl.multiple_of(r * piece, piece), piece)

    def span(t, halo):
        first = max(0, mine * t - halo)
        last = min(height, mine * t + mine + halo)
        return first, last - first, first - (mine * t - halo)

    moves = []
    for source, target, halo, send, recv, esend, erecv in (
        (x_ref, xf, 2, x_send, x_recv, xe_send, xe_recv),
        (f_ref, ff, 1, f_send, f_recv, fe_send, fe_recv),
    ):
        up = remote(
            source.at[pl.ds(height - halo, halo)], target.at[pl.ds(0, halo), columns],
            esend.at[0], erecv.at[r], {"mode": m + 1, "rank": 0},
        )
        down = remote(
            source.at[pl.ds(0, halo)], target.at[pl.ds(mine + halo, halo), columns],
            esend.at[1], erecv.at[r], {"mode": m - 1, "rank": nr - 1},
        )
        pl.when(has_next)(up.start)
        pl.when(has_prev)(down.start)
        across = []
        for t in range(nr):
            first, count, offset = span(t, halo)
            copy = remote(
                source.at[pl.ds(first, count)], target.at[pl.ds(offset, count), columns],
                send.at[t], recv.at[r], at_r(t),
            )
            pl.when(r != t)(copy.start)
            across.append(copy)
        moves.append((up, down, across))
        if source is x_ref:
            c_up = remote(
                c_ref.at[pl.ds(height - 1, 1)], ce.at[pl.ds(0, 1)],
                ce_send.at[0], ce_recv.at[0], {"mode": m + 1, "rank": r},
            )
            c_down = remote(
                c_ref.at[pl.ds(0, 1)], ce.at[pl.ds(mine + 1, 1)],
                ce_send.at[1], ce_recv.at[1], {"mode": m - 1, "rank": r},
            )
            pl.when((r == 0) & has_next)(c_up.start)
            pl.when((r == nr - 1) & has_prev)(c_down.start)

    for t in range(nr):

        @pl.when(r == t)
        def _():
            for source, target, halo, sem in (
                (x_ref, xf, 2, own_sem.at[2]), (f_ref, ff, 1, own_sem.at[3])
            ):
                first, count, offset = span(t, halo)
                pltpu.make_async_copy(
                    source.at[pl.ds(first, count)],
                    target.at[pl.ds(offset, count), pl.ds(t * piece, piece)],
                    sem,
                ).start()
            first, count, offset = span(t, 1)
            ce[offset : offset + count] = c_ref[first : first + count]

    @pl.when((r == 0) & jnp.logical_not(has_prev))
    def _():
        xf[0:2] = jnp.zeros((2, width, width), F32)
        ff[0:1] = jnp.zeros((1, width, width), F32)
        ce[0:1] = jnp.zeros((1,) + ce.shape[1:], F32)

    @pl.when((r == nr - 1) & jnp.logical_not(has_next))
    def _():
        xf[mine + 2 :] = jnp.zeros((2, width, width), F32)
        ff[mine + 1 :] = jnp.zeros((1, width, width), F32)
        ce[mine + 1 :] = jnp.zeros((1,) + ce.shape[1:], F32)

    fetch_l.wait()
    for k in range(3):
        turned = l_ref[k].T
        lt_rows[k * width : (k + 1) * width, :] = turned
        lt_cols[:, k * width : (k + 1) * width] = turned

    low_edge = (r == 0) & has_prev
    high_edge = (r == nr - 1) & has_next

    def arrive(target, halo, recv, erecv, send, esend, own):
        for t in range(nr):
            part = pl.ds(t * piece, piece)
            _, count, offset = span(t, halo)
            block = target.at[pl.ds(offset, count), part]
            pl.when(r == t)(pltpu.make_async_copy(block, block, own).wait)
            for mine_rank in range(nr):
                if mine_rank == t:
                    continue
                _, count, offset = span(mine_rank, halo)
                block = target.at[pl.ds(offset, count), part]
                pl.when(r == mine_rank)(
                    remote(block, block, send.at[t], recv.at[t], at_r(t)).wait_recv
                )
            block = target.at[pl.ds(0, halo), part]
            pl.when(low_edge)(remote(block, block, esend.at[0], erecv.at[t], at_r(t)).wait_recv)
            block = target.at[pl.ds(mine + halo, halo), part]
            pl.when(high_edge)(remote(block, block, esend.at[1], erecv.at[t], at_r(t)).wait_recv)

    arrive(xf, 2, x_recv, xe_recv, x_send, xe_send, own_sem.at[2])
    pl.when(low_edge)(c_up.wait_recv)
    pl.when(high_edge)(c_down.wait_recv)

    fetch_p.wait()
    contract_right(xf, p_ref, tt, mine + 4, width)
    arrive(ff, 1, f_recv, fe_recv, f_send, fe_send, own_sem.at[3])

    def applied(index, row):
        pair = coupled_pair(tt, ce, row, index, False, width)
        stacked = jnp.concatenate([jnp.concatenate(parts, axis=1) for parts in pair], axis=0)
        return dot(stacked, lt_rows[...])

    def residual_body(p, carry):
        out = applied(2 * p, 2 * p)
        res[2 * p] = ff[2 * p] - out[:width]
        res[2 * p + 1] = ff[2 * p + 1] - out[width:]
        return carry

    lax.fori_loop(0, (mine + 2) // 2, residual_body, 0)

    def gram_body(p, total):
        i = 2 * p
        both = jnp.concatenate(
            [
                jnp.concatenate([xf[i + 2], xf[i + 3]], axis=1),
                jnp.concatenate([res[i + 1], res[i + 2]], axis=1),
            ],
            axis=0,
        )
        return total + dot(both, both, ((1,), (1,)))

    total = lax.fori_loop(0, mine // 2, gram_body, jnp.zeros((2 * width, 2 * width), F32))
    cross = total[:width, width:]
    pieces = jnp.concatenate(
        [total[:width, :width], cross + cross.T, total[width:, width:]], axis=0
    )
    gpart[...] = pieces.reshape(gpart.shape)

    def scatter(part, recv_buf, send, recv):
        for d in range(1, na):
            t = lax.rem(g + d, na)
            remote(part.at[t], recv_buf.at[g], send.at[d - 1], recv.at[d - 1], at_a(t)).start()
        recv_buf[g] = part[g]

    def spread(part, recv_buf, send, recv):
        for d in range(1, na):
            t = lax.rem(g + d, na)
            remote(part, recv_buf.at[g], send.at[d - 1], recv.at[d - 1], at_a(t)).start()
        recv_buf[g] = part[...]

    def gathered(recv_buf, send, recv):
        for d in range(1, na):
            t = lax.rem(g + na - d, na)
            block = recv_buf.at[t]
            remote(block, block, send.at[d - 1], recv.at[d - 1], at_a(t)).wait_recv()

    def exchange_b(part, recv_buf, send, recv):
        for d in range(1, mh):
            t = lax.rem(high + d, mh)
            remote(part, recv_buf.at[high], send.at[d - 1], recv.at[d - 1], at_b(t)).start()
        recv_buf[high] = part[...]

    def gathered_b(recv_buf, send, recv):
        for d in range(1, mh):
            t = lax.rem(high + mh - d, mh)
            block = recv_buf.at[t]
            remote(block, block, send.at[d - 1], recv.at[d - 1], at_b(t)).wait_recv()

    def add_up(recv_buf, count):
        out = recv_buf[0]
        for t in range(1, count):
            out = out + recv_buf[t]
        return out

    scatter(gpart, grecv, ga_send, ga_recv)
    contract_right(res, p_ref, tt, mine + 2, width)
    gathered(grecv, ga_send, ga_recv)
    gsend[...] = add_up(grecv, na)
    exchange_b(gsend, gbrecv, gb_send, gb_recv)

    def fold(values):
        return jnp.sum(values.reshape(width // 8, 8, width), axis=0)

    def image_body(p, carry):
        along, energy = carry
        image = applied(2 * p, 2 * p + 1)
        along = along + fold(res[2 * p + 1] * image[:width])
        along = along + fold(res[2 * p + 2] * image[width:])
        return along, energy + fold(image[:width] * image[:width] + image[width:] * image[width:])

    zero = jnp.zeros((8, width), F32)
    along, energy = lax.fori_loop(0, mine // 2, image_body, (zero, zero))
    ssend[0:1, :] = jnp.sum(along, axis=0, keepdims=True)
    ssend[1:2, :] = jnp.sum(energy, axis=0, keepdims=True)
    ssend[2:8, :] = jnp.zeros((6, width), F32)
    spread(ssend, srecv, sa_send, sa_recv)
    gathered_b(gbrecv, gb_send, gb_recv)
    gfull[g] = add_up(gbrecv, mh)
    for d in range(1, na):
        t = lax.rem(g + d, na)
        remote(gfull.at[g], gfull.at[g], gc_send.at[d - 1], gc_recv.at[d - 1], at_a(t)).start()
    gathered(srecv, sa_send, sa_recv)
    sbsend[...] = add_up(srecv, na)
    exchange_b(sbsend, sbrecv, sb_send, sb_recv)
    gathered(gfull, gc_send, gc_recv)
    gathered_b(sbrecv, sb_send, sb_recv)
    sums = jnp.sum(add_up(sbrecv, mh), axis=1, keepdims=True)
    alpha = sums[0:1, :] / sums[1:2, :]

    grams = gfull[...].reshape(3 * width, width)
    gram = (
        grams[:width] + alpha * grams[width : 2 * width] + (alpha * alpha) * grams[2 * width :]
    ) * scale
    rows = lax.broadcasted_iota(jnp.int32, (width, width), 0)
    lanes = lax.broadcasted_iota(jnp.int32, (width, width), 1)
    work[:, :width] = gram
    work[:, width:] = jnp.where(rows == lanes, 1.0, 0.0).astype(F32)
    eliminate(work, width)
    tri_out[...] = jnp.where(lanes >= rows, work[:, :width], 0.0)
    inverse = jnp.where(lanes <= rows, work[:, width:], 0.0)

    def basis_body(p, carry):
        pair = jnp.concatenate(
            [xf[2 * p + 1] + alpha * res[2 * p], xf[2 * p + 2] + alpha * res[2 * p + 1]], axis=1
        )
        out = dot(inverse, pair)
        qb[2 * p] = out[:, :width]
        qb[2 * p + 1] = out[:, width:]
        return carry

    lax.fori_loop(0, (mine + 2) // 2, basis_body, 0)
    slab = pl.ds(r * mine, mine)
    for d in range(1, nr):
        t = lax.rem(r + d, nr)
        remote(
            qb.at[pl.ds(1, mine), pl.ds(pl.multiple_of(t * piece, piece), piece)],
            q_out.at[slab], q_send.at[d - 1], q_recv.at[d - 1], at_r(t),
        ).start()

    def mixed_body(p, carry):
        out = dot(jnp.concatenate([qb[2 * p], qb[2 * p + 1]], axis=0), lt_cols[...])
        for k in range(3):
            tt[k, 2 * p] = out[:width, k * width : (k + 1) * width]
            tt[k, 2 * p + 1] = out[width:, k * width : (k + 1) * width]
        return carry

    lax.fori_loop(0, (mine + 2) // 2, mixed_body, 0)

    def interface_body(p, total):
        i = 2 * p
        pair = coupled_pair(tt, ce, i + 1, i, True, width)
        moved = jnp.concatenate([jnp.concatenate(parts, axis=0) for parts in pair], axis=1)
        basis = jnp.concatenate([qb[i + 1], qb[i + 2]], axis=1)
        return total + dot(moved, basis, ((1,), (1,)))

    total = lax.fori_loop(0, mine // 2, interface_body, jnp.zeros((3 * width, width), F32)) * scale
    total = total.reshape(3, nr, piece, width)
    for t in range(nr):
        npart[t * ml : (t + 1) * ml] = total[:, t].reshape((ml,) + npart.shape[1:])
    scatter(npart, nrecv, na_send, na_recv)
    q_out[slab] = qb[1 : mine + 1, columns, :]
    gathered(nrecv, na_send, na_recv)
    nsend[...] = add_up(nrecv, na)
    exchange_b(nsend, nbrecv, nb_send, nb_recv)
    gathered_b(nbrecv, nb_send, nb_recv)
    nfull[low] = add_up(nbrecv, mh)

    def at_c(t):
        return {"mode": high * ml + t, "rank": r}

    for d in range(1, ml):
        t = lax.rem(low + d, ml)
        remote(
            nfull.at[low], nfull.at[low], nc_send.at[d - 1], nc_recv.at[d - 1], at_c(t)
        ).start()
    for d in range(1, ml):
        t = lax.rem(low + ml - d, ml)
        block = nfull.at[t]
        remote(block, block, nc_send.at[d - 1], nc_recv.at[d - 1], at_c(t)).wait_recv()
    n_out[...] = nfull[...]

    for d in range(1, nr):
        t = lax.rem(r + nr - d, nr)
        block = q_out.at[pl.ds(t * mine, mine)]
        remote(block, block, q_send.at[d - 1], q_recv.at[d - 1], at_r(t)).wait_recv()

    for up, down, across in moves:
        pl.when(has_next)(up.wait_send)
        pl.when(has_prev)(down.wait_send)
        for t in range(nr):
            pl.when(r != t)(across[t].wait_send)
    pl.when((r == 0) & has_next)(c_up.wait_send)
    pl.when((r == nr - 1) & has_prev)(c_down.wait_send)
    for send, block, count in (
        (ga_send, gpart.at[0], na), (gc_send, gfull.at[0], na), (sa_send, ssend, na),
        (na_send, npart.at[0], na), (gb_send, gsend, mh), (sb_send, sbsend, mh),
        (nb_send, nsend, mh), (nc_send, nfull.at[0], ml), (q_send, q_out.at[pl.ds(0, mine)], nr),
    ):
        for d in range(1, count):
            remote(block, block, send.at[d - 1], send.at[d - 1], at_r(r)).wait_send()


def shards(nm, nr, start_core, right_side, left_interface, right_interface, couplings):
    height, piece, width = start_core.shape
    mine = height // nr
    ml = max(1, min(nm, 8 // nr))
    mh = nm // ml
    na = nr * ml
    scale = 1.0 / (height * nm * width)
    grows = 3 * width // na
    nrows = 3 * piece // ml
    vmem = lambda *shape: pltpu.VMEM(shape, F32)
    sem = lambda count: pltpu.SemaphoreType.DMA((max(1, count),))
    scratch = [
        vmem(3, width, width), vmem(3 * width, width), vmem(height, 27, width), sem(4),
        vmem(mine + 4, width, width), vmem(mine + 2, width, width), vmem(mine + 2, 27, width),
        vmem(3, mine + 4, width, width), vmem(mine + 2, width, width),
        vmem(mine + 2, width, width), vmem(3 * width, width), vmem(width, 3 * width),
        vmem(width, 2 * width),
        vmem(na, grows, width), vmem(na, grows, width), vmem(grows, width),
        vmem(mh, grows, width), vmem(na, grows, width),
        vmem(8, width), vmem(na, 8, width), vmem(8, width), vmem(mh, 8, width),
        vmem(na, nrows, width), vmem(na, nrows, width), vmem(nrows, width),
        vmem(mh, nrows, width), vmem(ml, nrows, width),
        sem(nr), sem(nr), sem(2), sem(nr),
        sem(nr), sem(nr), sem(2), sem(nr),
        sem(2), sem(2),
        sem(na), sem(na), sem(mh), sem(mh), sem(na), sem(na),
        sem(na), sem(na), sem(mh), sem(mh),
        sem(na), sem(na), sem(mh), sem(mh), sem(ml), sem(ml),
        sem(nr), sem(nr),
    ]
    space = pl.BlockSpec(memory_space=pltpu.VMEM)
    basis, triangle, interface = pl.pallas_call(
        functools.partial(kernel, nm, nr, ml, scale),
        out_shape=(
            jax.ShapeDtypeStruct((height, piece, width), F32),
            jax.ShapeDtypeStruct((width, width), F32),
            jax.ShapeDtypeStruct((ml, nrows, width), F32),
        ),
        in_specs=[pl.BlockSpec(memory_space=pl.ANY)] * 4 + [space],
        out_specs=(space,) * 3,
        scratch_shapes=scratch,
        compiler_params=pltpu.CompilerParams(
            collective_id=0, has_side_effects=True, vmem_limit_bytes=40 * 1024 * 1024
        ),
    )(
        start_core, right_side, left_interface,
        right_interface.reshape(3 * width, width), couplings,
    )
    return basis, triangle, interface.reshape(3, piece, width)


def solution(mesh):
    placed = (
        P("mode", "rank", None),
        P("mode", "rank", None),
        P(),
        P(),
        P(None, None, None, "mode"),
    )
    return jax.shard_map(
        functools.partial(shards, mesh.shape["mode"], mesh.shape["rank"]),
        mesh=mesh,
        in_specs=placed,
        out_specs=(P("mode", "rank", None), P(), P(None, "rank", None)),
        check_vma=False,
    )
```

```python
import functools

import jax
import jax.numpy as jnp
from jax import lax
from jax.experimental import pallas as pl
from jax.experimental.pallas import tpu as pltpu
from jax.sharding import PartitionSpec as P

HIGH = lax.Precision.HIGH
F32 = jnp.float32


def dot(a, b, dims=((1,), (0,)), precision=HIGH):
    return lax.dot_general(a, b, (dims, ((), ())), precision=precision, preferred_element_type=F32)


def contract_right(source, weights, target, count, width):
    def body(p, carry):
        pair = jnp.concatenate([source[2 * p], source[2 * p + 1]], axis=1)
        out = dot(weights[...], pair)
        for k in range(3):
            rows = out[k * width : (k + 1) * width]
            target[k, 2 * p] = rows[:, :width]
            target[k, 2 * p + 1] = rows[:, width:]
        return carry

    lax.fori_loop(0, count // 2, body, 0)


def coupled(field, factors, row, index, inner_first, width):
    step = min(64, width)
    pieces = []
    for start in range(0, width, step):
        sums = [None] * 3
        for k in range(3):
            for s in range(3):
                block = field[k, index + s, start : start + step, :]
                for o in range(3):
                    pair = (k * 3 + o) if inner_first else (o * 3 + k)
                    term = factors[row, pl.ds(pair * 3 + s, 1), :] * block
                    sums[o] = term if sums[o] is None else sums[o] + term
        pieces.append(sums)
    return [jnp.concatenate([piece[o] for piece in pieces], axis=0) for o in range(3)]


def coupled_pair(field, factors, row, index, inner_first, width):
    return [coupled(field, factors, row + d, index + d, inner_first, width) for d in range(2)]


def eliminate(work, width):
    size = 8
    sub = lax.broadcasted_iota(jnp.int32, (size, 2 * width), 0)
    for k in range(width // size):
        base = k * size
        panel = work[base : base + size, :]
        rows = [jnp.broadcast_to(panel[i : i + 1, :], (size, 2 * width)) for i in range(size)]
        entry, factors, inverses = {}, {}, []
        for j in range(size):
            column = jnp.broadcast_to(panel[:, base + j : base + j + 1], (size, width))
            for i in range(j, size):
                entry[i, j] = jnp.broadcast_to(column[i : i + 1, :], (size, width))
        for j in range(size):
            pivot = entry[j, j]
            inv = lax.rsqrt(pivot)
            inv = inv * (1.5 - 0.5 * (pivot * inv) * inv)
            rows[j] = rows[j] * jnp.concatenate([inv, inv], axis=1)
            inverses.append(inv)
            scaled = {i: entry[i, j] * inv for i in range(j + 1, size)}
            for i in scaled:
                factors[i, j] = scaled[i]
            for c in range(j + 1, size):
                for i in range(c, size):
                    entry[i, c] = entry[i, c] - scaled[i] * scaled[c]
            for i in range(j + 1, size):
                factor = jnp.concatenate([scaled[i], scaled[i]], axis=1)
                rows[i] = rows[i] - factor * rows[j]
        done = rows[0]
        for i in range(1, size):
            done = jnp.where(sub == i, rows[i], done)
        work[base : base + size, :] = done
        for start in range(base + size, width, size):
            block = work[start : start + size, :]
            lower = []
            for j in range(size):
                column = jnp.broadcast_to(block[:, base + j : base + j + 1], (size, width))
                for c in range(j):
                    column = column - lower[c] * factors[j, c]
                lower.append(column * inverses[j])
            for j in range(size):
                block = block - jnp.concatenate([lower[j], lower[j]], axis=1) * rows[j]
            work[start : start + size, :] = block


def kernel(
    nm, nr, ml, scale,
    x_ref, f_ref, l_hbm, p_hbm, raw_ref,
    q_out, tri_out, n_out,
    l_ref, p_ref, c_ref, own_sem,
    xf, ff, ce, tt, res, qb, lt_rows, lt_cols, work,
    gpart, grecv, gsend, gbrecv, gfull,
    ssend, srecv, sbsend, sbrecv,
    npart, nrecv, nsend, nbrecv, nfull,
    x_send, x_recv, xe_send, xe_recv,
    f_send, f_recv, fe_send, fe_recv,
    ce_send, ce_recv,
    ga_send, ga_recv, gb_send, gb_recv, gc_send, gc_recv,
    sa_send, sa_recv, sb_send, sb_recv,
    na_send, na_recv, nb_send, nb_recv, nc_send, nc_recv,
    q_send, q_recv,
):
    height, piece, width = x_ref.shape
    mine = height // nr
    mh = nm // ml
    na = nr * ml
    m = lax.axis_index("mode")
    r = lax.axis_index("rank")
    low = lax.rem(m, ml)
    high = lax.div(m, ml)
    g = r * ml + low
    has_prev = m > 0
    has_next = m < nm - 1

    def at_a(t):
        return {"mode": high * ml + lax.rem(t, ml), "rank": lax.div(t, ml)}

    def at_b(t):
        return {"mode": t * ml + low, "rank": r}

    def at_r(t):
        return {"mode": m, "rank": t}

    def remote(src, dst, send, recv, where):
        return pltpu.make_async_remote_copy(
            src_ref=src, dst_ref=dst, send_sem=send, recv_sem=recv,
            device_id=where, device_id_type=pl.DeviceIdType.MESH,
        )

    def greet(where):
        pl.semaphore_signal(
            barrier, inc=1, device_id=where, device_id_type=pl.DeviceIdType.MESH
        )

    fetch_l = pltpu.make_async_copy(l_hbm, l_ref, own_sem.at[0])
    fetch_p = pltpu.make_async_copy(p_hbm, p_ref, own_sem.at[1])
    fetch_l.start()
    fetch_p.start()

    barrier = pltpu.get_barrier_semaphore()
    for d in range(1, na):
        greet(at_a(lax.rem(g + d, na)))
    for d in range(1, mh):
        greet(at_b(lax.rem(high + d, mh)))

    @pl.when(has_prev)
    def _():
        for t in range(nr):
            greet({"mode": m - 1, "rank": t})

    @pl.when(has_next)
    def _():
        for t in range(nr):
            greet({"mode": m + 1, "rank": t})

    for o in range(3):
        for k in range(3):
            block = raw_ref[o, k]
            first = (o * 3 + k) * 3
            for i in range(height):
                c_ref[i, first : first + 3, :] = jnp.broadcast_to(block[:, i : i + 1], (3, width))

    pl.semaphore_wait(
        barrier, na - 1 + mh - 1 + nr * (has_prev.astype(jnp.int32) + has_next.astype(jnp.int32))
    )

    columns = pl.ds(pl.multiple_of(r * piece, piece), piece)

    def span(t, halo):
        first = max(0, mine * t - halo)
        last = min(height, mine * t + mine + halo)
        return first, last - first, first - (mine * t - halo)

    moves = []
    for source, target, halo, send, recv, esend, erecv in (
        (x_ref, xf, 2, x_send, x_recv, xe_send, xe_recv),
        (f_ref, ff, 1, f_send, f_recv, fe_send, fe_recv),
    ):
        up = remote(
            source.at[pl.ds(height - halo, halo)], target.at[pl.ds(0, halo), columns],
            esend.at[0], erecv.at[r], {"mode": m + 1, "rank": 0},
        )
        down = remote(
            source.at[pl.ds(0, halo)], target.at[pl.ds(mine + halo, halo), columns],
            esend.at[1], erecv.at[r], {"mode": m - 1, "rank": nr - 1},
        )
        pl.when(has_next)(up.start)
        pl.when(has_prev)(down.start)
        across = []
        for t in range(nr):
            first, count, offset = span(t, halo)
            copy = remote(
                source.at[pl.ds(first, count)], target.at[pl.ds(offset, count), columns],
                send.at[t], recv.at[r], at_r(t),
            )
            pl.when(r != t)(copy.start)
            across.append(copy)
        moves.append((up, down, across))
        if source is x_ref:
            c_up = remote(
                c_ref.at[pl.ds(height - 1, 1)], ce.at[pl.ds(0, 1)],
                ce_send.at[0], ce_recv.at[0], {"mode": m + 1, "rank": r},
            )
            c_down = remote(
                c_ref.at[pl.ds(0, 1)], ce.at[pl.ds(mine + 1, 1)],
                ce_send.at[1], ce_recv.at[1], {"mode": m - 1, "rank": r},
            )
            pl.when((r == 0) & has_next)(c_up.start)
            pl.when((r == nr - 1) & has_prev)(c_down.start)

    for t in range(nr):

        @pl.when(r == t)
        def _():
            for source, target, halo, sem in (
                (x_ref, xf, 2, own_sem.at[2]), (f_ref, ff, 1, own_sem.at[3])
            ):
                first, count, offset = span(t, halo)
                pltpu.make_async_copy(
                    source.at[pl.ds(first, count)],
                    target.at[pl.ds(offset, count), pl.ds(t * piece, piece)],
                    sem,
                ).start()
            first, count, offset = span(t, 1)
            ce[offset : offset + count] = c_ref[first : first + count]

    @pl.when((r == 0) & jnp.logical_not(has_prev))
    def _():
        xf[0:2] = jnp.zeros((2, width, width), F32)
        ff[0:1] = jnp.zeros((1, width, width), F32)
        ce[0:1] = jnp.zeros((1,) + ce.shape[1:], F32)

    @pl.when((r == nr - 1) & jnp.logical_not(has_next))
    def _():
        xf[mine + 2 :] = jnp.zeros((2, width, width), F32)
        ff[mine + 1 :] = jnp.zeros((1, width, width), F32)
        ce[mine + 1 :] = jnp.zeros((1,) + ce.shape[1:], F32)

    fetch_l.wait()
    for k in range(3):
        turned = l_ref[k].T
        lt_rows[k * width : (k + 1) * width, :] = turned
        lt_cols[:, k * width : (k + 1) * width] = turned

    low_edge = (r == 0) & has_prev
    high_edge = (r == nr - 1) & has_next

    def arrive(target, halo, recv, erecv, send, esend, own):
        for t in range(nr):
            part = pl.ds(t * piece, piece)
            _, count, offset = span(t, halo)
            block = target.at[pl.ds(offset, count), part]
            pl.when(r == t)(pltpu.make_async_copy(block, block, own).wait)
            for mine_rank in range(nr):
                if mine_rank == t:
                    continue
                _, count, offset = span(mine_rank, halo)
                block = target.at[pl.ds(offset, count), part]
                pl.when(r == mine_rank)(
                    remote(block, block, send.at[t], recv.at[t], at_r(t)).wait_recv
                )
            block = target.at[pl.ds(0, halo), part]
            pl.when(low_edge)(remote(block, block, esend.at[0], erecv.at[t], at_r(t)).wait_recv)
            block = target.at[pl.ds(mine + halo, halo), part]
            pl.when(high_edge)(remote(block, block, esend.at[1], erecv.at[t], at_r(t)).wait_recv)

    arrive(xf, 2, x_recv, xe_recv, x_send, xe_send, own_sem.at[2])
    pl.when(low_edge)(c_up.wait_recv)
    pl.when(high_edge)(c_down.wait_recv)

    fetch_p.wait()
    contract_right(xf, p_ref, tt, mine + 4, width)

    def applied(index, row):
        pair = coupled_pair(tt, ce, row, index, False, width)
        stacked = jnp.concatenate([jnp.concatenate(parts, axis=1) for parts in pair], axis=0)
        return dot(stacked, lt_rows[...])

    def applied_body(p, carry):
        out = applied(2 * p, 2 * p)
        res[2 * p] = out[:width]
        res[2 * p + 1] = out[width:]
        return carry

    lax.fori_loop(0, (mine + 2) // 2, applied_body, 0)
    arrive(ff, 1, f_recv, fe_recv, f_send, fe_send, own_sem.at[3])
    res[...] = ff[...] - res[...]

    def gram_body(p, total):
        i = 2 * p
        both = jnp.concatenate(
            [
                jnp.concatenate([xf[i + 2], xf[i + 3]], axis=1),
                jnp.concatenate([res[i + 1], res[i + 2]], axis=1),
            ],
            axis=0,
        )
        return total + dot(both, both, ((1,), (1,)))

    total = lax.fori_loop(0, mine // 2, gram_body, jnp.zeros((2 * width, 2 * width), F32))
    cross = total[:width, width:]
    pieces = jnp.concatenate(
        [total[:width, :width], cross + cross.T, total[width:, width:]], axis=0
    )
    gpart[...] = pieces.reshape(gpart.shape)

    def scatter(part, recv_buf, send, recv):
        for d in range(1, na):
            t = lax.rem(g + d, na)
            remote(part.at[t], recv_buf.at[g], send.at[d - 1], recv.at[d - 1], at_a(t)).start()
        recv_buf[g] = part[g]

    def spread(part, recv_buf, send, recv):
        for d in range(1, na):
            t = lax.rem(g + d, na)
            remote(part, recv_buf.at[g], send.at[d - 1], recv.at[d - 1], at_a(t)).start()
        recv_buf[g] = part[...]

    def gathered(recv_buf, send, recv):
        for d in range(1, na):
            t = lax.rem(g + na - d, na)
            block = recv_buf.at[t]
            remote(block, block, send.at[d - 1], recv.at[d - 1], at_a(t)).wait_recv()

    def exchange_b(part, recv_buf, send, recv):
        for d in range(1, mh):
            t = lax.rem(high + d, mh)
            remote(part, recv_buf.at[high], send.at[d - 1], recv.at[d - 1], at_b(t)).start()
        recv_buf[high] = part[...]

    def gathered_b(recv_buf, send, recv):
        for d in range(1, mh):
            t = lax.rem(high + mh - d, mh)
            block = recv_buf.at[t]
            remote(block, block, send.at[d - 1], recv.at[d - 1], at_b(t)).wait_recv()

    def add_up(recv_buf, count):
        out = recv_buf[0]
        for t in range(1, count):
            out = out + recv_buf[t]
        return out

    scatter(gpart, grecv, ga_send, ga_recv)
    contract_right(res, p_ref, tt, mine + 2, width)
    gathered(grecv, ga_send, ga_recv)
    gsend[...] = add_up(grecv, na)
    exchange_b(gsend, gbrecv, gb_send, gb_recv)

    def fold(values):
        return jnp.sum(values.reshape(width // 8, 8, width), axis=0)

    def image_body(p, carry):
        along, energy = carry
        image = applied(2 * p, 2 * p + 1)
        along = along + fold(res[2 * p + 1] * image[:width])
        along = along + fold(res[2 * p + 2] * image[width:])
        return along, energy + fold(image[:width] * image[:width] + image[width:] * image[width:])

    zero = jnp.zeros((8, width), F32)
    along, energy = lax.fori_loop(0, mine // 2, image_body, (zero, zero))
    ssend[0:1, :] = jnp.sum(along, axis=0, keepdims=True)
    ssend[1:2, :] = jnp.sum(energy, axis=0, keepdims=True)
    ssend[2:8, :] = jnp.zeros((6, width), F32)
    spread(ssend, srecv, sa_send, sa_recv)
    gathered_b(gbrecv, gb_send, gb_recv)
    gfull[g] = add_up(gbrecv, mh)
    for d in range(1, na):
        t = lax.rem(g + d, na)
        remote(gfull.at[g], gfull.at[g], gc_send.at[d - 1], gc_recv.at[d - 1], at_a(t)).start()
    gathered(srecv, sa_send, sa_recv)
    sbsend[...] = add_up(srecv, na)
    exchange_b(sbsend, sbrecv, sb_send, sb_recv)
    gathered(gfull, gc_send, gc_recv)
    gathered_b(sbrecv, sb_send, sb_recv)
    sums = jnp.sum(add_up(sbrecv, mh), axis=1, keepdims=True)
    alpha = sums[0:1, :] / sums[1:2, :]

    grams = gfull[...].reshape(3 * width, width)
    gram = (
        grams[:width] + alpha * grams[width : 2 * width] + (alpha * alpha) * grams[2 * width :]
    ) * scale
    rows = lax.broadcasted_iota(jnp.int32, (width, width), 0)
    lanes = lax.broadcasted_iota(jnp.int32, (width, width), 1)
    work[:, :width] = gram
    work[:, width:] = jnp.where(rows == lanes, 1.0, 0.0).astype(F32)
    eliminate(work, width)
    tri_out[...] = jnp.where(lanes >= rows, work[:, :width], 0.0)
    inverse = jnp.where(lanes <= rows, work[:, width:], 0.0)

    def basis_body(p, carry):
        pair = jnp.concatenate(
            [xf[2 * p + 1] + alpha * res[2 * p], xf[2 * p + 2] + alpha * res[2 * p + 1]], axis=1
        )
        out = dot(inverse, pair)
        qb[2 * p] = out[:, :width]
        qb[2 * p + 1] = out[:, width:]
        return carry

    lax.fori_loop(0, (mine + 2) // 2, basis_body, 0)
    slab = pl.ds(r * mine, mine)
    for d in range(1, nr):
        t = lax.rem(r + d, nr)
        remote(
            qb.at[pl.ds(1, mine), pl.ds(pl.multiple_of(t * piece, piece), piece)],
            q_out.at[slab], q_send.at[d - 1], q_recv.at[d - 1], at_r(t),
        ).start()

    def mixed_body(p, carry):
        out = dot(jnp.concatenate([qb[2 * p], qb[2 * p + 1]], axis=0), lt_cols[...])
        for k in range(3):
            tt[k, 2 * p] = out[:width, k * width : (k + 1) * width]
            tt[k, 2 * p + 1] = out[width:, k * width : (k + 1) * width]
        return carry

    lax.fori_loop(0, (mine + 2) // 2, mixed_body, 0)

    def interface_body(p, total):
        i = 2 * p
        pair = coupled_pair(tt, ce, i + 1, i, True, width)
        moved = jnp.concatenate([jnp.concatenate(parts, axis=0) for parts in pair], axis=1)
        basis = jnp.concatenate([qb[i + 1], qb[i + 2]], axis=1)
        return total + dot(moved, basis, ((1,), (1,)))

    total = lax.fori_loop(0, mine // 2, interface_body, jnp.zeros((3 * width, width), F32)) * scale
    total = total.reshape(3, nr, piece, width)
    for t in range(nr):
        npart[t * ml : (t + 1) * ml] = total[:, t].reshape((ml,) + npart.shape[1:])
    scatter(npart, nrecv, na_send, na_recv)
    q_out[slab] = qb[1 : mine + 1, columns, :]
    gathered(nrecv, na_send, na_recv)
    nsend[...] = add_up(nrecv, na)
    exchange_b(nsend, nbrecv, nb_send, nb_recv)
    gathered_b(nbrecv, nb_send, nb_recv)
    nfull[low] = add_up(nbrecv, mh)

    def at_c(t):
        return {"mode": high * ml + t, "rank": r}

    for d in range(1, ml):
        t = lax.rem(low + d, ml)
        remote(
            nfull.at[low], nfull.at[low], nc_send.at[d - 1], nc_recv.at[d - 1], at_c(t)
        ).start()
    for d in range(1, ml):
        t = lax.rem(low + ml - d, ml)
        block = nfull.at[t]
        remote(block, block, nc_send.at[d - 1], nc_recv.at[d - 1], at_c(t)).wait_recv()
    n_out[...] = nfull[...]

    for d in range(1, nr):
        t = lax.rem(r + nr - d, nr)
        block = q_out.at[pl.ds(t * mine, mine)]
        remote(block, block, q_send.at[d - 1], q_recv.at[d - 1], at_r(t)).wait_recv()

    for up, down, across in moves:
        pl.when(has_next)(up.wait_send)
        pl.when(has_prev)(down.wait_send)
        for t in range(nr):
            pl.when(r != t)(across[t].wait_send)
    pl.when((r == 0) & has_next)(c_up.wait_send)
    pl.when((r == nr - 1) & has_prev)(c_down.wait_send)
    for send, block, count in (
        (ga_send, gpart.at[0], na), (gc_send, gfull.at[0], na), (sa_send, ssend, na),
        (na_send, npart.at[0], na), (gb_send, gsend, mh), (sb_send, sbsend, mh),
        (nb_send, nsend, mh), (nc_send, nfull.at[0], ml), (q_send, q_out.at[pl.ds(0, mine)], nr),
    ):
        for d in range(1, count):
            remote(block, block, send.at[d - 1], send.at[d - 1], at_r(r)).wait_send()


def shards(nm, nr, start_core, right_side, left_interface, right_interface, couplings):
    height, piece, width = start_core.shape
    mine = height // nr
    ml = max(1, min(nm, 8 // nr))
    mh = nm // ml
    na = nr * ml
    scale = 1.0 / (height * nm * width)
    grows = 3 * width // na
    nrows = 3 * piece // ml
    vmem = lambda *shape: pltpu.VMEM(shape, F32)
    sem = lambda count: pltpu.SemaphoreType.DMA((max(1, count),))
    scratch = [
        vmem(3, width, width), vmem(3 * width, width), vmem(height, 27, width), sem(4),
        vmem(mine + 4, width, width), vmem(mine + 2, width, width), vmem(mine + 2, 27, width),
        vmem(3, mine + 4, width, width), vmem(mine + 2, width, width),
        vmem(mine + 2, width, width), vmem(3 * width, width), vmem(width, 3 * width),
        vmem(width, 2 * width),
        vmem(na, grows, width), vmem(na, grows, width), vmem(grows, width),
        vmem(mh, grows, width), vmem(na, grows, width),
        vmem(8, width), vmem(na, 8, width), vmem(8, width), vmem(mh, 8, width),
        vmem(na, nrows, width), vmem(na, nrows, width), vmem(nrows, width),
        vmem(mh, nrows, width), vmem(ml, nrows, width),
        sem(nr), sem(nr), sem(2), sem(nr),
        sem(nr), sem(nr), sem(2), sem(nr),
        sem(2), sem(2),
        sem(na), sem(na), sem(mh), sem(mh), sem(na), sem(na),
        sem(na), sem(na), sem(mh), sem(mh),
        sem(na), sem(na), sem(mh), sem(mh), sem(ml), sem(ml),
        sem(nr), sem(nr),
    ]
    space = pl.BlockSpec(memory_space=pltpu.VMEM)
    basis, triangle, interface = pl.pallas_call(
        functools.partial(kernel, nm, nr, ml, scale),
        out_shape=(
            jax.ShapeDtypeStruct((height, piece, width), F32),
            jax.ShapeDtypeStruct((width, width), F32),
            jax.ShapeDtypeStruct((ml, nrows, width), F32),
        ),
        in_specs=[pl.BlockSpec(memory_space=pltpu.HBM)] * 4 + [space],
        out_specs=(space,) * 3,
        scratch_shapes=scratch,
        compiler_params=pltpu.CompilerParams(
            collective_id=0, has_side_effects=True, vmem_limit_bytes=60 * 1024 * 1024
        ),
    )(
        start_core, right_side, left_interface,
        right_interface.reshape(3 * width, width), couplings,
    )
    return basis, triangle, interface.reshape(3, piece, width)


def solution(mesh):
    placed = (
        P("mode", "rank", None),
        P("mode", "rank", None),
        P(),
        P(),
        P(None, None, None, "mode"),
    )
    return jax.shard_map(
        functools.partial(shards, mesh.shape["mode"], mesh.shape["rank"]),
        mesh=mesh,
        in_specs=placed,
        out_specs=(P("mode", "rank", None), P(), P(None, "rank", None)),
        check_vma=False,
    )
```

```python
import functools

import jax
import jax.numpy as jnp
from jax import lax
from jax.experimental import pallas as pl
from jax.experimental.pallas import tpu as pltpu
from jax.sharding import PartitionSpec as P

HIGH = lax.Precision.HIGH
HIGHEST = lax.Precision.HIGHEST
F32 = jnp.float32


def dot(a, b, dims=((1,), (0,)), precision=HIGH):
    return lax.dot_general(a, b, (dims, ((), ())), precision=precision, preferred_element_type=F32)


def contract_right(source, weights, target, count, width):
    def body(p, carry):
        pair = jnp.concatenate([source[2 * p], source[2 * p + 1]], axis=1)
        out = dot(weights[...], pair)
        for k in range(3):
            rows = out[k * width : (k + 1) * width]
            target[k, 2 * p] = rows[:, :width]
            target[k, 2 * p + 1] = rows[:, width:]
        return carry

    lax.fori_loop(0, count // 2, body, 0)


def coupled(field, factors, row, index, inner_first, width):
    step = min(64, width)
    pieces = []
    for start in range(0, width, step):
        sums = [None] * 3
        for k in range(3):
            for s in range(3):
                block = field[k, index + s, start : start + step, :]
                for o in range(3):
                    pair = (k * 3 + o) if inner_first else (o * 3 + k)
                    term = factors[row, pl.ds(pair * 3 + s, 1), :] * block
                    sums[o] = term if sums[o] is None else sums[o] + term
        pieces.append(sums)
    return [jnp.concatenate([piece[o] for piece in pieces], axis=0) for o in range(3)]


def coupled_pair(field, factors, row, index, inner_first, width):
    return [coupled(field, factors, row + d, index + d, inner_first, width) for d in range(2)]


def eliminate(work, width, begin, end):
    size = 8
    sub = lax.broadcasted_iota(jnp.int32, (size, 2 * width), 0)
    for k in range(begin, end):
        base = k * size
        panel = work[base : base + size, :]
        rows = [jnp.broadcast_to(panel[i : i + 1, :], (size, 2 * width)) for i in range(size)]
        entry, factors, inverses = {}, {}, []
        for j in range(size):
            column = jnp.broadcast_to(panel[:, base + j : base + j + 1], (size, width))
            for i in range(j, size):
                entry[i, j] = jnp.broadcast_to(column[i : i + 1, :], (size, width))
        for j in range(size):
            pivot = entry[j, j]
            inv = lax.rsqrt(pivot)
            inv = inv * (1.5 - 0.5 * (pivot * inv) * inv)
            rows[j] = rows[j] * jnp.concatenate([inv, inv], axis=1)
            inverses.append(inv)
            scaled = {i: entry[i, j] * inv for i in range(j + 1, size)}
            for i in scaled:
                factors[i, j] = scaled[i]
            for c in range(j + 1, size):
                for i in range(c, size):
                    entry[i, c] = entry[i, c] - scaled[i] * scaled[c]
            for i in range(j + 1, size):
                factor = jnp.concatenate([scaled[i], scaled[i]], axis=1)
                rows[i] = rows[i] - factor * rows[j]
        done = rows[0]
        for i in range(1, size):
            done = jnp.where(sub == i, rows[i], done)
        work[base : base + size, :] = done
        for start in range(base + size, width, size):
            block = work[start : start + size, :]
            lower = []
            for j in range(size):
                column = jnp.broadcast_to(block[:, base + j : base + j + 1], (size, width))
                for c in range(j):
                    column = column - lower[c] * factors[j, c]
                lower.append(column * inverses[j])
            for j in range(size):
                block = block - jnp.concatenate([lower[j], lower[j]], axis=1) * rows[j]
            work[start : start + size, :] = block


def kernel(
    nm, nr, ml, scale,
    x_ref, f_ref, l_hbm, p_hbm, raw_ref,
    q_out, tri_out, n_out,
    l_ref, p_ref, c_ref, own_sem,
    xf, ff, ce, tt, res, qb, cfull, lt_rows, lt_cols, work,
    gpart, grecv, gsend, gbrecv, gfull,
    ssend, srecv, sbsend, sbrecv,
    npart, nrecv, nsend, nbrecv, nfull,
    x_send, x_recv, xe_send, xe_recv,
    f_send, f_recv, fe_send, fe_recv,
    ce_send, ce_recv,
    ga_send, ga_recv, gb_send, gb_recv, gc_send, gc_recv,
    sa_send, sa_recv, sb_send, sb_recv,
    na_send, na_recv, nb_send, nb_recv, nc_send, nc_recv,
    q_send, q_recv,
):
    height, piece, width = x_ref.shape
    mine = height // nr
    mh = nm // ml
    na = nr * ml
    m = lax.axis_index("mode")
    r = lax.axis_index("rank")
    low = lax.rem(m, ml)
    high = lax.div(m, ml)
    g = r * ml + low
    has_prev = m > 0
    has_next = m < nm - 1

    def at_a(t):
        return {"mode": high * ml + lax.rem(t, ml), "rank": lax.div(t, ml)}

    def at_b(t):
        return {"mode": t * ml + low, "rank": r}

    def at_r(t):
        return {"mode": m, "rank": t}

    def remote(src, dst, send, recv, where):
        return pltpu.make_async_remote_copy(
            src_ref=src, dst_ref=dst, send_sem=send, recv_sem=recv,
            device_id=where, device_id_type=pl.DeviceIdType.MESH,
        )

    def greet(where):
        pl.semaphore_signal(
            barrier, inc=1, device_id=where, device_id_type=pl.DeviceIdType.MESH
        )

    fetch_l = pltpu.make_async_copy(l_hbm, l_ref, own_sem.at[0])
    fetch_p = pltpu.make_async_copy(p_hbm, p_ref, own_sem.at[1])
    fetch_l.start()
    fetch_p.start()

    barrier = pltpu.get_barrier_semaphore()
    for d in range(1, na):
        greet(at_a(lax.rem(g + d, na)))
    for d in range(1, mh):
        greet(at_b(lax.rem(high + d, mh)))

    @pl.when(has_prev)
    def _():
        for t in range(nr):
            greet({"mode": m - 1, "rank": t})

    @pl.when(has_next)
    def _():
        for t in range(nr):
            greet({"mode": m + 1, "rank": t})

    for o in range(3):
        for k in range(3):
            block = raw_ref[o, k]
            first = (o * 3 + k) * 3
            for i in range(height):
                c_ref[i, first : first + 3, :] = jnp.broadcast_to(block[:, i : i + 1], (3, width))

    pl.semaphore_wait(
        barrier, na - 1 + mh - 1 + nr * (has_prev.astype(jnp.int32) + has_next.astype(jnp.int32))
    )

    columns = pl.ds(pl.multiple_of(r * piece, piece), piece)

    def span(t, halo):
        first = max(0, mine * t - halo)
        last = min(height, mine * t + mine + halo)
        return first, last - first, first - (mine * t - halo)

    moves = []
    for source, target, halo, send, recv, esend, erecv in (
        (x_ref, xf, 2, x_send, x_recv, xe_send, xe_recv),
        (f_ref, ff, 1, f_send, f_recv, fe_send, fe_recv),
    ):
        up = remote(
            source.at[pl.ds(height - halo, halo)], target.at[pl.ds(0, halo), columns],
            esend.at[0], erecv.at[r], {"mode": m + 1, "rank": 0},
        )
        down = remote(
            source.at[pl.ds(0, halo)], target.at[pl.ds(mine + halo, halo), columns],
            esend.at[1], erecv.at[r], {"mode": m - 1, "rank": nr - 1},
        )
        pl.when(has_next)(up.start)
        pl.when(has_prev)(down.start)
        across = []
        for t in range(nr):
            first, count, offset = span(t, halo)
            copy = remote(
                source.at[pl.ds(first, count)], target.at[pl.ds(offset, count), columns],
                send.at[t], recv.at[r], at_r(t),
            )
            pl.when(r != t)(copy.start)
            across.append(copy)
        moves.append((up, down, across))
        if source is x_ref:
            c_up = remote(
                c_ref.at[pl.ds(height - 1, 1)], ce.at[pl.ds(0, 1)],
                ce_send.at[0], ce_recv.at[0], {"mode": m + 1, "rank": r},
            )
            c_down = remote(
                c_ref.at[pl.ds(0, 1)], ce.at[pl.ds(mine + 1, 1)],
                ce_send.at[1], ce_recv.at[1], {"mode": m - 1, "rank": r},
            )
            pl.when((r == 0) & has_next)(c_up.start)
            pl.when((r == nr - 1) & has_prev)(c_down.start)

    for t in range(nr):

        @pl.when(r == t)
        def _():
            for source, target, halo, sem in (
                (x_ref, xf, 2, own_sem.at[2]), (f_ref, ff, 1, own_sem.at[3])
            ):
                first, count, offset = span(t, halo)
                pltpu.make_async_copy(
                    source.at[pl.ds(first, count)],
                    target.at[pl.ds(offset, count), pl.ds(t * piece, piece)],
                    sem,
                ).start()
            first, count, offset = span(t, 1)
            ce[offset : offset + count] = c_ref[first : first + count]

    @pl.when((r == 0) & jnp.logical_not(has_prev))
    def _():
        xf[0:2] = jnp.zeros((2, width, width), F32)
        ff[0:1] = jnp.zeros((1, width, width), F32)
        ce[0:1] = jnp.zeros((1,) + ce.shape[1:], F32)

    @pl.when((r == nr - 1) & jnp.logical_not(has_next))
    def _():
        xf[mine + 2 :] = jnp.zeros((2, width, width), F32)
        ff[mine + 1 :] = jnp.zeros((1, width, width), F32)
        ce[mine + 1 :] = jnp.zeros((1,) + ce.shape[1:], F32)

    fetch_l.wait()
    for k in range(3):
        turned = l_ref[k].T
        lt_rows[k * width : (k + 1) * width, :] = turned
        lt_cols[:, k * width : (k + 1) * width] = turned

    low_edge = (r == 0) & has_prev
    high_edge = (r == nr - 1) & has_next

    def arrive(target, halo, recv, erecv, send, esend, own):
        for t in range(nr):
            part = pl.ds(t * piece, piece)
            _, count, offset = span(t, halo)
            block = target.at[pl.ds(offset, count), part]
            pl.when(r == t)(pltpu.make_async_copy(block, block, own).wait)
            for mine_rank in range(nr):
                if mine_rank == t:
                    continue
                _, count, offset = span(mine_rank, halo)
                block = target.at[pl.ds(offset, count), part]
                pl.when(r == mine_rank)(
                    remote(block, block, send.at[t], recv.at[t], at_r(t)).wait_recv
                )
            block = target.at[pl.ds(0, halo), part]
            pl.when(low_edge)(remote(block, block, esend.at[0], erecv.at[t], at_r(t)).wait_recv)
            block = target.at[pl.ds(mine + halo, halo), part]
            pl.when(high_edge)(remote(block, block, esend.at[1], erecv.at[t], at_r(t)).wait_recv)

    arrive(xf, 2, x_recv, xe_recv, x_send, xe_send, own_sem.at[2])
    pl.when(low_edge)(c_up.wait_recv)
    pl.when(high_edge)(c_down.wait_recv)

    fetch_p.wait()
    contract_right(xf, p_ref, tt, mine + 4, width)

    def applied(index, row):
        pair = coupled_pair(tt, ce, row, index, False, width)
        stacked = jnp.concatenate([jnp.concatenate(parts, axis=1) for parts in pair], axis=0)
        return dot(stacked, lt_rows[...])

    def applied_body(p, carry):
        out = applied(2 * p, 2 * p)
        res[2 * p] = out[:width]
        res[2 * p + 1] = out[width:]
        return carry

    lax.fori_loop(0, (mine + 2) // 2, applied_body, 0)
    arrive(ff, 1, f_recv, fe_recv, f_send, fe_send, own_sem.at[3])
    res[...] = ff[...] - res[...]

    def gram_body(p, total):
        i = 2 * p
        both = jnp.concatenate(
            [
                jnp.concatenate([xf[i + 2], xf[i + 3]], axis=1),
                jnp.concatenate([res[i + 1], res[i + 2]], axis=1),
            ],
            axis=0,
        )
        return total + dot(both, both, ((1,), (1,)))

    total = lax.fori_loop(0, mine // 2, gram_body, jnp.zeros((2 * width, 2 * width), F32))
    cross = total[:width, width:]
    pieces = jnp.concatenate(
        [total[:width, :width], cross + cross.T, total[width:, width:]], axis=0
    )
    gpart[...] = pieces.reshape(gpart.shape)

    def scatter(part, recv_buf, send, recv):
        for d in range(1, na):
            t = lax.rem(g + d, na)
            remote(part.at[t], recv_buf.at[g], send.at[d - 1], recv.at[d - 1], at_a(t)).start()
        recv_buf[g] = part[g]

    def spread(part, recv_buf, send, recv):
        for d in range(1, na):
            t = lax.rem(g + d, na)
            remote(part, recv_buf.at[g], send.at[d - 1], recv.at[d - 1], at_a(t)).start()
        recv_buf[g] = part[...]

    def gathered(recv_buf, send, recv):
        for d in range(1, na):
            t = lax.rem(g + na - d, na)
            block = recv_buf.at[t]
            remote(block, block, send.at[d - 1], recv.at[d - 1], at_a(t)).wait_recv()

    def exchange_b(part, recv_buf, send, recv):
        for d in range(1, mh):
            t = lax.rem(high + d, mh)
            remote(part, recv_buf.at[high], send.at[d - 1], recv.at[d - 1], at_b(t)).start()
        recv_buf[high] = part[...]

    def gathered_b(recv_buf, send, recv):
        for d in range(1, mh):
            t = lax.rem(high + mh - d, mh)
            block = recv_buf.at[t]
            remote(block, block, send.at[d - 1], recv.at[d - 1], at_b(t)).wait_recv()

    def add_up(recv_buf, count):
        out = recv_buf[0]
        for t in range(1, count):
            out = out + recv_buf[t]
        return out

    scatter(gpart, grecv, ga_send, ga_recv)
    contract_right(res, p_ref, tt, mine + 2, width)
    gathered(grecv, ga_send, ga_recv)
    gsend[...] = add_up(grecv, na)
    exchange_b(gsend, gbrecv, gb_send, gb_recv)

    def fold(values):
        return jnp.sum(values.reshape(width // 8, 8, width), axis=0)

    def image_body(p, carry):
        along, energy = carry
        image = applied(2 * p, 2 * p + 1)
        along = along + fold(res[2 * p + 1] * image[:width])
        along = along + fold(res[2 * p + 2] * image[width:])
        return along, energy + fold(image[:width] * image[:width] + image[width:] * image[width:])

    zero = jnp.zeros((8, width), F32)
    along, energy = lax.fori_loop(0, mine // 2, image_body, (zero, zero))
    ssend[0:1, :] = jnp.sum(along, axis=0, keepdims=True)
    ssend[1:2, :] = jnp.sum(energy, axis=0, keepdims=True)
    ssend[2:8, :] = jnp.zeros((6, width), F32)
    spread(ssend, srecv, sa_send, sa_recv)
    gathered_b(gbrecv, gb_send, gb_recv)
    gfull[g] = add_up(gbrecv, mh)
    for d in range(1, na):
        t = lax.rem(g + d, na)
        remote(gfull.at[g], gfull.at[g], gc_send.at[d - 1], gc_recv.at[d - 1], at_a(t)).start()
    gathered(srecv, sa_send, sa_recv)
    sbsend[...] = add_up(srecv, na)
    exchange_b(sbsend, sbrecv, sb_send, sb_recv)
    gathered(gfull, gc_send, gc_recv)
    gathered_b(sbrecv, sb_send, sb_recv)
    sums = jnp.sum(add_up(sbrecv, mh), axis=1, keepdims=True)
    alpha = sums[0:1, :] / sums[1:2, :]

    grams = gfull[...].reshape(3 * width, width)
    gram = (
        grams[:width] + alpha * grams[width : 2 * width] + (alpha * alpha) * grams[2 * width :]
    ) * scale
    rows = lax.broadcasted_iota(jnp.int32, (width, width), 0)
    lanes = lax.broadcasted_iota(jnp.int32, (width, width), 1)
    work[:, :width] = gram
    work[:, width:] = jnp.where(rows == lanes, 1.0, 0.0).astype(F32)
    def core_body(i, carry):
        qb[i] = xf[i + 1] + alpha * res[i]
        return carry

    lax.fori_loop(0, mine + 2, core_body, 0)
    slab = pl.ds(r * mine, mine)
    for d in range(1, nr):
        t = lax.rem(r + d, nr)
        remote(
            qb.at[pl.ds(1, mine)], cfull.at[slab], q_send.at[d - 1], q_recv.at[d - 1], at_r(t)
        ).start()

    def mixed_body(p, carry):
        out = dot(jnp.concatenate([qb[2 * p], qb[2 * p + 1]], axis=0), lt_cols[...])
        for k in range(3):
            tt[k, 2 * p] = out[:width, k * width : (k + 1) * width]
            tt[k, 2 * p + 1] = out[width:, k * width : (k + 1) * width]
        return carry

    lax.fori_loop(0, (mine + 2) // 2, mixed_body, 0)

    def interface_body(p, total):
        i = 2 * p
        pair = coupled_pair(tt, ce, i + 1, i, True, width)
        moved = jnp.concatenate([jnp.concatenate(parts, axis=0) for parts in pair], axis=1)
        fields = jnp.concatenate([qb[i + 1], qb[i + 2]], axis=1)
        return total + dot(moved, fields, ((1,), (1,)))

    total = lax.fori_loop(0, mine // 2, interface_body, jnp.zeros((3 * width, width), F32)) * scale
    npart[...] = total.reshape(npart.shape)
    scatter(npart, nrecv, na_send, na_recv)
    cfull[slab] = qb[1 : mine + 1]

    blocks = width // 8
    stops = [0, blocks * 3 // 8, blocks * 5 // 8, blocks]
    eliminate(work, width, stops[0], stops[1])
    gathered(nrecv, na_send, na_recv)
    nsend[...] = add_up(nrecv, na)
    exchange_b(nsend, nbrecv, nb_send, nb_recv)
    eliminate(work, width, stops[1], stops[2])
    gathered_b(nbrecv, nb_send, nb_recv)
    nfull[g] = add_up(nbrecv, mh)
    for d in range(1, na):
        t = lax.rem(g + d, na)
        remote(nfull.at[g], nfull.at[g], nc_send.at[d - 1], nc_recv.at[d - 1], at_a(t)).start()
    eliminate(work, width, stops[2], stops[3])
    tri_out[...] = jnp.where(lanes >= rows, work[:, :width], 0.0)
    inverse = jnp.where(lanes <= rows, work[:, width:], 0.0)
    work[:, width:] = inverse
    owned = work[columns, width:]

    for d in range(1, nr):
        t = lax.rem(r + nr - d, nr)
        block = cfull.at[pl.ds(t * mine, mine)]
        remote(block, block, q_send.at[d - 1], q_recv.at[d - 1], at_r(t)).wait_recv()

    def basis_body(p, carry):
        out = dot(owned, jnp.concatenate([cfull[2 * p], cfull[2 * p + 1]], axis=1))
        q_out[2 * p] = out[:, :width]
        q_out[2 * p + 1] = out[:, width:]
        return carry

    lax.fori_loop(0, height // 2, basis_body, 0)
    gathered(nfull, nc_send, nc_recv)
    sums = nfull[...].reshape(3 * width, width)
    for k in range(3):
        half = dot(owned, sums[k * width : (k + 1) * width], precision=HIGHEST)
        n_out[k] = dot(half, inverse, ((1,), (1,)), HIGHEST)

    for up, down, across in moves:
        pl.when(has_next)(up.wait_send)
        pl.when(has_prev)(down.wait_send)
        for t in range(nr):
            pl.when(r != t)(across[t].wait_send)
    pl.when((r == 0) & has_next)(c_up.wait_send)
    pl.when((r == nr - 1) & has_prev)(c_down.wait_send)
    for send, block, count in (
        (ga_send, gpart.at[0], na), (gc_send, gfull.at[0], na), (sa_send, ssend, na),
        (na_send, npart.at[0], na), (gb_send, gsend, mh), (sb_send, sbsend, mh),
        (nb_send, nsend, mh), (nc_send, nfull.at[0], na), (q_send, cfull.at[pl.ds(0, mine)], nr),
    ):
        for d in range(1, count):
            remote(block, block, send.at[d - 1], send.at[d - 1], at_r(r)).wait_send()


def shards(nm, nr, start_core, right_side, left_interface, right_interface, couplings):
    height, piece, width = start_core.shape
    mine = height // nr
    ml = max(1, min(nm, 8 // nr))
    mh = nm // ml
    na = nr * ml
    scale = 1.0 / (height * nm * width)
    grows = 3 * width // na
    vmem = lambda *shape: pltpu.VMEM(shape, F32)
    sem = lambda count: pltpu.SemaphoreType.DMA((max(1, count),))
    scratch = [
        vmem(3, width, width), vmem(3 * width, width), vmem(height, 27, width), sem(4),
        vmem(mine + 4, width, width), vmem(mine + 2, width, width), vmem(mine + 2, 27, width),
        vmem(3, mine + 4, width, width), vmem(mine + 2, width, width),
        vmem(mine + 2, width, width), vmem(height, width, width),
        vmem(3 * width, width), vmem(width, 3 * width),
        vmem(width, 2 * width),
        vmem(na, grows, width), vmem(na, grows, width), vmem(grows, width),
        vmem(mh, grows, width), vmem(na, grows, width),
        vmem(8, width), vmem(na, 8, width), vmem(8, width), vmem(mh, 8, width),
        vmem(na, grows, width), vmem(na, grows, width), vmem(grows, width),
        vmem(mh, grows, width), vmem(na, grows, width),
        sem(nr), sem(nr), sem(2), sem(nr),
        sem(nr), sem(nr), sem(2), sem(nr),
        sem(2), sem(2),
        sem(na), sem(na), sem(mh), sem(mh), sem(na), sem(na),
        sem(na), sem(na), sem(mh), sem(mh),
        sem(na), sem(na), sem(mh), sem(mh), sem(na), sem(na),
        sem(nr), sem(nr),
    ]
    space = pl.BlockSpec(memory_space=pltpu.VMEM)
    basis, triangle, interface = pl.pallas_call(
        functools.partial(kernel, nm, nr, ml, scale),
        out_shape=(
            jax.ShapeDtypeStruct((height, piece, width), F32),
            jax.ShapeDtypeStruct((width, width), F32),
            jax.ShapeDtypeStruct((3, piece, width), F32),
        ),
        in_specs=[pl.BlockSpec(memory_space=pltpu.HBM)] * 4 + [space],
        out_specs=(space,) * 3,
        scratch_shapes=scratch,
        compiler_params=pltpu.CompilerParams(
            collective_id=0, has_side_effects=True, vmem_limit_bytes=60 * 1024 * 1024
        ),
    )(
        start_core, right_side, left_interface,
        right_interface.reshape(3 * width, width), couplings,
    )
    return basis, triangle, interface


def solution(mesh):
    placed = (
        P("mode", "rank", None),
        P("mode", "rank", None),
        P(),
        P(),
        P(None, None, None, "mode"),
    )
    return jax.shard_map(
        functools.partial(shards, mesh.shape["mode"], mesh.shape["rank"]),
        mesh=mesh,
        in_specs=placed,
        out_specs=(P("mode", "rank", None), P(), P(None, "rank", None)),
        check_vma=False,
    )
```

```python
import functools

import jax
import jax.numpy as jnp
from jax import lax
from jax.experimental import pallas as pl
from jax.experimental.pallas import tpu as pltpu
from jax.sharding import PartitionSpec as P

HIGH = lax.Precision.HIGH
HIGHEST = lax.Precision.HIGHEST
F32 = jnp.float32


def dot(a, b, dims=((1,), (0,)), precision=HIGH):
    return lax.dot_general(a, b, (dims, ((), ())), precision=precision, preferred_element_type=F32)


def contract_right(source, weights, target, count, width):
    def body(p, carry):
        pair = jnp.concatenate([source[2 * p], source[2 * p + 1]], axis=1)
        out = dot(weights[...], pair)
        for k in range(3):
            rows = out[k * width : (k + 1) * width]
            target[k, 2 * p] = rows[:, :width]
            target[k, 2 * p + 1] = rows[:, width:]
        return carry

    lax.fori_loop(0, count // 2, body, 0)


def coupled(field, factors, row, index, inner_first, width):
    step = min(64, width)
    pieces = []
    for start in range(0, width, step):
        sums = [None] * 3
        for k in range(3):
            for s in range(3):
                block = field[k, index + s, start : start + step, :]
                for o in range(3):
                    pair = (k * 3 + o) if inner_first else (o * 3 + k)
                    term = factors[row, pl.ds(pair * 3 + s, 1), :] * block
                    sums[o] = term if sums[o] is None else sums[o] + term
        pieces.append(sums)
    return [jnp.concatenate([piece[o] for piece in pieces], axis=0) for o in range(3)]


def coupled_pair(field, factors, row, index, inner_first, width):
    return [coupled(field, factors, row + d, index + d, inner_first, width) for d in range(2)]


def eliminate(work, width, begin, end):
    size = 8
    sub = lax.broadcasted_iota(jnp.int32, (size, 2 * width), 0)
    for k in range(begin, end):
        base = k * size
        panel = work[base : base + size, :]
        rows = [jnp.broadcast_to(panel[i : i + 1, :], (size, 2 * width)) for i in range(size)]
        entry, factors, inverses = {}, {}, []
        for j in range(size):
            column = jnp.broadcast_to(panel[:, base + j : base + j + 1], (size, width))
            for i in range(j, size):
                entry[i, j] = jnp.broadcast_to(column[i : i + 1, :], (size, width))
        for j in range(size):
            pivot = entry[j, j]
            inv = lax.rsqrt(pivot)
            inv = inv * (1.5 - 0.5 * (pivot * inv) * inv)
            rows[j] = rows[j] * jnp.concatenate([inv, inv], axis=1)
            inverses.append(inv)
            scaled = {i: entry[i, j] * inv for i in range(j + 1, size)}
            for i in scaled:
                factors[i, j] = scaled[i]
            for c in range(j + 1, size):
                for i in range(c, size):
                    entry[i, c] = entry[i, c] - scaled[i] * scaled[c]
            for i in range(j + 1, size):
                factor = jnp.concatenate([scaled[i], scaled[i]], axis=1)
                rows[i] = rows[i] - factor * rows[j]
        done = rows[0]
        for i in range(1, size):
            done = jnp.where(sub == i, rows[i], done)
        work[base : base + size, :] = done
        for start in range(base + size, width, size):
            block = work[start : start + size, :]
            lower = []
            for j in range(size):
                column = jnp.broadcast_to(block[:, base + j : base + j + 1], (size, width))
                for c in range(j):
                    column = column - lower[c] * factors[j, c]
                lower.append(column * inverses[j])
            for j in range(size):
                block = block - jnp.concatenate([lower[j], lower[j]], axis=1) * rows[j]
            work[start : start + size, :] = block


def kernel(
    nm, nr, ml, scale,
    x_ref, f_ref, l_hbm, p_hbm, raw_ref,
    q_out, tri_out, n_out,
    l_ref, p_ref, c_ref, own_sem,
    xf, ff, ce, tt, res, qb, cfull, qlate, lt_rows, lt_cols, work,
    gpart, grecv, gsend, gbrecv, gfull,
    ssend, srecv, sbsend, sbrecv,
    npart, nrecv, nsend, nbrecv, nfull,
    x_send, x_recv, xe_send, xe_recv,
    f_send, f_recv, fe_send, fe_recv,
    ce_send, ce_recv,
    ga_send, ga_recv, gb_send, gb_recv, gc_send, gc_recv,
    sa_send, sa_recv, sb_send, sb_recv,
    na_send, na_recv, nb_send, nb_recv, nc_send, nc_recv,
    q_send, q_recv, e_send, e_recv,
):
    height, piece, width = x_ref.shape
    mine = height // nr
    mh = nm // ml
    na = nr * ml
    m = lax.axis_index("mode")
    r = lax.axis_index("rank")
    low = lax.rem(m, ml)
    high = lax.div(m, ml)
    g = r * ml + low
    has_prev = m > 0
    has_next = m < nm - 1

    def at_a(t):
        return {"mode": high * ml + lax.rem(t, ml), "rank": lax.div(t, ml)}

    def at_b(t):
        return {"mode": t * ml + low, "rank": r}

    def at_r(t):
        return {"mode": m, "rank": t}

    def remote(src, dst, send, recv, where):
        return pltpu.make_async_remote_copy(
            src_ref=src, dst_ref=dst, send_sem=send, recv_sem=recv,
            device_id=where, device_id_type=pl.DeviceIdType.MESH,
        )

    def greet(where):
        pl.semaphore_signal(
            barrier, inc=1, device_id=where, device_id_type=pl.DeviceIdType.MESH
        )

    fetch_l = pltpu.make_async_copy(l_hbm, l_ref, own_sem.at[0])
    fetch_p = pltpu.make_async_copy(p_hbm, p_ref, own_sem.at[1])
    fetch_l.start()
    fetch_p.start()

    barrier = pltpu.get_barrier_semaphore()
    for d in range(1, na):
        greet(at_a(lax.rem(g + d, na)))
    for d in range(1, mh):
        greet(at_b(lax.rem(high + d, mh)))

    @pl.when(has_prev)
    def _():
        for t in range(nr):
            greet({"mode": m - 1, "rank": t})

    @pl.when(has_next)
    def _():
        for t in range(nr):
            greet({"mode": m + 1, "rank": t})

    for o in range(3):
        for k in range(3):
            block = raw_ref[o, k]
            first = (o * 3 + k) * 3
            for i in range(height):
                c_ref[i, first : first + 3, :] = jnp.broadcast_to(block[:, i : i + 1], (3, width))

    pl.semaphore_wait(
        barrier, na - 1 + mh - 1 + nr * (has_prev.astype(jnp.int32) + has_next.astype(jnp.int32))
    )

    columns = pl.ds(pl.multiple_of(r * piece, piece), piece)

    def span(t, halo):
        first = max(0, mine * t - halo)
        last = min(height, mine * t + mine + halo)
        return first, last - first, first - (mine * t - halo)

    moves = []
    for source, target, halo, send, recv, esend, erecv in (
        (x_ref, xf, 2, x_send, x_recv, xe_send, xe_recv),
        (f_ref, ff, 1, f_send, f_recv, fe_send, fe_recv),
    ):
        up = remote(
            source.at[pl.ds(height - halo, halo)], target.at[pl.ds(0, halo), columns],
            esend.at[0], erecv.at[r], {"mode": m + 1, "rank": 0},
        )
        down = remote(
            source.at[pl.ds(0, halo)], target.at[pl.ds(mine + halo, halo), columns],
            esend.at[1], erecv.at[r], {"mode": m - 1, "rank": nr - 1},
        )
        pl.when(has_next)(up.start)
        pl.when(has_prev)(down.start)
        across = []
        for t in range(nr):
            first, count, offset = span(t, halo)
            copy = remote(
                source.at[pl.ds(first, count)], target.at[pl.ds(offset, count), columns],
                send.at[t], recv.at[r], at_r(t),
            )
            pl.when(r != t)(copy.start)
            across.append(copy)
        moves.append((up, down, across))
        if source is x_ref:
            c_up = remote(
                c_ref.at[pl.ds(height - 1, 1)], ce.at[pl.ds(0, 1)],
                ce_send.at[0], ce_recv.at[0], {"mode": m + 1, "rank": r},
            )
            c_down = remote(
                c_ref.at[pl.ds(0, 1)], ce.at[pl.ds(mine + 1, 1)],
                ce_send.at[1], ce_recv.at[1], {"mode": m - 1, "rank": r},
            )
            pl.when((r == 0) & has_next)(c_up.start)
            pl.when((r == nr - 1) & has_prev)(c_down.start)

    for t in range(nr):

        @pl.when(r == t)
        def _():
            for source, target, halo, sem in (
                (x_ref, xf, 2, own_sem.at[2]), (f_ref, ff, 1, own_sem.at[3])
            ):
                first, count, offset = span(t, halo)
                pltpu.make_async_copy(
                    source.at[pl.ds(first, count)],
                    target.at[pl.ds(offset, count), pl.ds(t * piece, piece)],
                    sem,
                ).start()
            first, count, offset = span(t, 1)
            ce[offset : offset + count] = c_ref[first : first + count]

    @pl.when((r == 0) & jnp.logical_not(has_prev))
    def _():
        xf[0:2] = jnp.zeros((2, width, width), F32)
        ff[0:1] = jnp.zeros((1, width, width), F32)
        ce[0:1] = jnp.zeros((1,) + ce.shape[1:], F32)

    @pl.when((r == nr - 1) & jnp.logical_not(has_next))
    def _():
        xf[mine + 2 :] = jnp.zeros((2, width, width), F32)
        ff[mine + 1 :] = jnp.zeros((1, width, width), F32)
        ce[mine + 1 :] = jnp.zeros((1,) + ce.shape[1:], F32)

    fetch_l.wait()
    for k in range(3):
        turned = l_ref[k].T
        lt_rows[k * width : (k + 1) * width, :] = turned
        lt_cols[:, k * width : (k + 1) * width] = turned

    low_edge = (r == 0) & has_prev
    high_edge = (r == nr - 1) & has_next

    def arrive(target, halo, recv, erecv, send, esend, own):
        for t in range(nr):
            part = pl.ds(t * piece, piece)
            _, count, offset = span(t, halo)
            block = target.at[pl.ds(offset, count), part]
            pl.when(r == t)(pltpu.make_async_copy(block, block, own).wait)
            for mine_rank in range(nr):
                if mine_rank == t:
                    continue
                _, count, offset = span(mine_rank, halo)
                block = target.at[pl.ds(offset, count), part]
                pl.when(r == mine_rank)(
                    remote(block, block, send.at[t], recv.at[t], at_r(t)).wait_recv
                )
            block = target.at[pl.ds(0, halo), part]
            pl.when(low_edge)(remote(block, block, esend.at[0], erecv.at[t], at_r(t)).wait_recv)
            block = target.at[pl.ds(mine + halo, halo), part]
            pl.when(high_edge)(remote(block, block, esend.at[1], erecv.at[t], at_r(t)).wait_recv)

    arrive(xf, 2, x_recv, xe_recv, x_send, xe_send, own_sem.at[2])
    pl.when(low_edge)(c_up.wait_recv)
    pl.when(high_edge)(c_down.wait_recv)

    fetch_p.wait()
    contract_right(xf, p_ref, tt, mine + 4, width)

    def applied(index, row):
        pair = coupled_pair(tt, ce, row, index, False, width)
        stacked = jnp.concatenate([jnp.concatenate(parts, axis=1) for parts in pair], axis=0)
        return dot(stacked, lt_rows[...])

    def applied_body(p, carry):
        out = applied(2 * p, 2 * p)
        res[2 * p] = out[:width]
        res[2 * p + 1] = out[width:]
        return carry

    lax.fori_loop(0, (mine + 2) // 2, applied_body, 0)
    arrive(ff, 1, f_recv, fe_recv, f_send, fe_send, own_sem.at[3])
    res[...] = ff[...] - res[...]

    def gram_body(p, total):
        i = 2 * p
        both = jnp.concatenate(
            [
                jnp.concatenate([xf[i + 2], xf[i + 3]], axis=1),
                jnp.concatenate([res[i + 1], res[i + 2]], axis=1),
            ],
            axis=0,
        )
        return total + dot(both, both, ((1,), (1,)))

    total = lax.fori_loop(0, mine // 2, gram_body, jnp.zeros((2 * width, 2 * width), F32))
    cross = total[:width, width:]
    pieces = jnp.concatenate(
        [total[:width, :width], cross + cross.T, total[width:, width:]], axis=0
    )
    gpart[...] = pieces.reshape(gpart.shape)

    def scatter(part, recv_buf, send, recv):
        for d in range(1, na):
            t = lax.rem(g + d, na)
            remote(part.at[t], recv_buf.at[g], send.at[d - 1], recv.at[d - 1], at_a(t)).start()
        recv_buf[g] = part[g]

    def spread(part, recv_buf, send, recv):
        for d in range(1, na):
            t = lax.rem(g + d, na)
            remote(part, recv_buf.at[g], send.at[d - 1], recv.at[d - 1], at_a(t)).start()
        recv_buf[g] = part[...]

    def gathered(recv_buf, send, recv):
        for d in range(1, na):
            t = lax.rem(g + na - d, na)
            block = recv_buf.at[t]
            remote(block, block, send.at[d - 1], recv.at[d - 1], at_a(t)).wait_recv()

    def exchange_b(part, recv_buf, send, recv):
        for d in range(1, mh):
            t = lax.rem(high + d, mh)
            remote(part, recv_buf.at[high], send.at[d - 1], recv.at[d - 1], at_b(t)).start()
        recv_buf[high] = part[...]

    def gathered_b(recv_buf, send, recv):
        for d in range(1, mh):
            t = lax.rem(high + mh - d, mh)
            block = recv_buf.at[t]
            remote(block, block, send.at[d - 1], recv.at[d - 1], at_b(t)).wait_recv()

    def add_up(recv_buf, count):
        out = recv_buf[0]
        for t in range(1, count):
            out = out + recv_buf[t]
        return out

    scatter(gpart, grecv, ga_send, ga_recv)
    contract_right(res, p_ref, tt, mine + 2, width)
    gathered(grecv, ga_send, ga_recv)
    gsend[...] = add_up(grecv, na)
    exchange_b(gsend, gbrecv, gb_send, gb_recv)

    def fold(values):
        return jnp.sum(values.reshape(width // 8, 8, width), axis=0)

    def image_body(p, carry):
        along, energy = carry
        image = applied(2 * p, 2 * p + 1)
        along = along + fold(res[2 * p + 1] * image[:width])
        along = along + fold(res[2 * p + 2] * image[width:])
        return along, energy + fold(image[:width] * image[:width] + image[width:] * image[width:])

    zero = jnp.zeros((8, width), F32)
    along, energy = lax.fori_loop(0, mine // 2, image_body, (zero, zero))
    ssend[0:1, :] = jnp.sum(along, axis=0, keepdims=True)
    ssend[1:2, :] = jnp.sum(energy, axis=0, keepdims=True)
    ssend[2:8, :] = jnp.zeros((6, width), F32)
    spread(ssend, srecv, sa_send, sa_recv)
    gathered_b(gbrecv, gb_send, gb_recv)
    gfull[g] = add_up(gbrecv, mh)
    for d in range(1, na):
        t = lax.rem(g + d, na)
        remote(gfull.at[g], gfull.at[g], gc_send.at[d - 1], gc_recv.at[d - 1], at_a(t)).start()
    gathered(srecv, sa_send, sa_recv)
    sbsend[...] = add_up(srecv, na)
    exchange_b(sbsend, sbrecv, sb_send, sb_recv)
    gathered(gfull, gc_send, gc_recv)
    gathered_b(sbrecv, sb_send, sb_recv)
    sums = jnp.sum(add_up(sbrecv, mh), axis=1, keepdims=True)
    alpha = sums[0:1, :] / sums[1:2, :]

    grams = gfull[...].reshape(3 * width, width)
    gram = (
        grams[:width] + alpha * grams[width : 2 * width] + (alpha * alpha) * grams[2 * width :]
    ) * scale
    rows = lax.broadcasted_iota(jnp.int32, (width, width), 0)
    lanes = lax.broadcasted_iota(jnp.int32, (width, width), 1)
    work[:, :width] = gram
    work[:, width:] = jnp.where(rows == lanes, 1.0, 0.0).astype(F32)
    def core_body(i, carry):
        qb[i] = xf[i + 1] + alpha * res[i]
        return carry

    lax.fori_loop(0, mine + 2, core_body, 0)
    early = cfull.shape[1]
    late = mine - early
    for d in range(1, nr):
        t = lax.rem(r + d, nr)
        remote(
            qb.at[pl.ds(1, early)], cfull.at[r], e_send.at[d - 1], e_recv.at[d - 1], at_r(t)
        ).start()

    def mixed_body(p, carry):
        out = dot(jnp.concatenate([qb[2 * p], qb[2 * p + 1]], axis=0), lt_cols[...])
        for k in range(3):
            tt[k, 2 * p] = out[:width, k * width : (k + 1) * width]
            tt[k, 2 * p + 1] = out[width:, k * width : (k + 1) * width]
        return carry

    lax.fori_loop(0, (mine + 2) // 2, mixed_body, 0)

    def interface_body(p, total):
        i = 2 * p
        pair = coupled_pair(tt, ce, i + 1, i, True, width)
        moved = jnp.concatenate([jnp.concatenate(parts, axis=0) for parts in pair], axis=1)
        fields = jnp.concatenate([qb[i + 1], qb[i + 2]], axis=1)
        return total + dot(moved, fields, ((1,), (1,)))

    total = lax.fori_loop(0, mine // 2, interface_body, jnp.zeros((3 * width, width), F32)) * scale
    npart[...] = total.reshape(npart.shape)
    scatter(npart, nrecv, na_send, na_recv)
    cfull[r] = qb[1 : early + 1]

    blocks = width // 8
    stops = [0, blocks * 3 // 8, blocks * 5 // 8, blocks]
    eliminate(work, width, stops[0], stops[1])
    gathered(nrecv, na_send, na_recv)
    nsend[...] = add_up(nrecv, na)
    exchange_b(nsend, nbrecv, nb_send, nb_recv)
    eliminate(work, width, stops[1], stops[2])
    gathered_b(nbrecv, nb_send, nb_recv)
    nfull[g] = add_up(nbrecv, mh)
    for d in range(1, na):
        t = lax.rem(g + d, na)
        remote(nfull.at[g], nfull.at[g], nc_send.at[d - 1], nc_recv.at[d - 1], at_a(t)).start()
    eliminate(work, width, stops[2], stops[3])
    tri_out[...] = jnp.where(lanes >= rows, work[:, :width], 0.0)
    inverse = jnp.where(lanes <= rows, work[:, width:], 0.0)
    work[:, width:] = inverse
    owned = work[columns, width:]

    for j in range(late):
        qlate[j] = dot(inverse, qb[early + 1 + j])
    own_late = pl.ds(r * mine + early, late)
    for d in range(1, nr):
        t = lax.rem(r + d, nr)
        remote(
            qlate.at[:, pl.ds(pl.multiple_of(t * piece, piece), piece)],
            q_out.at[own_late], q_send.at[d - 1], q_recv.at[d - 1], at_r(t),
        ).start()
    q_out[own_late] = qlate[:, columns, :]

    for d in range(1, nr):
        t = lax.rem(r + nr - d, nr)
        block = cfull.at[t]
        remote(block, block, e_send.at[d - 1], e_recv.at[d - 1], at_r(t)).wait_recv()
    for j in range(early):
        out = dot(owned, jnp.concatenate([cfull[t, j] for t in range(nr)], axis=1))
        for t in range(nr):
            q_out[t * mine + j] = out[:, t * width : (t + 1) * width]
    gathered(nfull, nc_send, nc_recv)
    sums = nfull[...].reshape(3 * width, width)
    for k in range(3):
        half = dot(owned, sums[k * width : (k + 1) * width], precision=HIGHEST)
        n_out[k] = dot(half, inverse, ((1,), (1,)), HIGHEST)

    for d in range(1, nr):
        t = lax.rem(r + nr - d, nr)
        block = q_out.at[pl.ds(t * mine + early, late)]
        remote(block, block, q_send.at[d - 1], q_recv.at[d - 1], at_r(t)).wait_recv()

    for up, down, across in moves:
        pl.when(has_next)(up.wait_send)
        pl.when(has_prev)(down.wait_send)
        for t in range(nr):
            pl.when(r != t)(across[t].wait_send)
    pl.when((r == 0) & has_next)(c_up.wait_send)
    pl.when((r == nr - 1) & has_prev)(c_down.wait_send)
    for send, block, count in (
        (ga_send, gpart.at[0], na), (gc_send, gfull.at[0], na), (sa_send, ssend, na),
        (na_send, npart.at[0], na), (gb_send, gsend, mh), (sb_send, sbsend, mh),
        (nb_send, nsend, mh), (nc_send, nfull.at[0], na), (q_send, q_out.at[pl.ds(0, late)], nr),
        (e_send, cfull.at[0], nr),
    ):
        for d in range(1, count):
            remote(block, block, send.at[d - 1], send.at[d - 1], at_r(r)).wait_send()


def shards(nm, nr, start_core, right_side, left_interface, right_interface, couplings):
    height, piece, width = start_core.shape
    mine = height // nr
    ml = max(1, min(nm, 8 // nr))
    mh = nm // ml
    na = nr * ml
    scale = 1.0 / (height * nm * width)
    grows = 3 * width // na
    vmem = lambda *shape: pltpu.VMEM(shape, F32)
    sem = lambda count: pltpu.SemaphoreType.DMA((max(1, count),))
    scratch = [
        vmem(3, width, width), vmem(3 * width, width), vmem(height, 27, width), sem(4),
        vmem(mine + 4, width, width), vmem(mine + 2, width, width), vmem(mine + 2, 27, width),
        vmem(3, mine + 4, width, width), vmem(mine + 2, width, width),
        vmem(mine + 2, width, width),
        vmem(nr, mine // 2, width, width), vmem(mine - mine // 2, width, width),
        vmem(3 * width, width), vmem(width, 3 * width),
        vmem(width, 2 * width),
        vmem(na, grows, width), vmem(na, grows, width), vmem(grows, width),
        vmem(mh, grows, width), vmem(na, grows, width),
        vmem(8, width), vmem(na, 8, width), vmem(8, width), vmem(mh, 8, width),
        vmem(na, grows, width), vmem(na, grows, width), vmem(grows, width),
        vmem(mh, grows, width), vmem(na, grows, width),
        sem(nr), sem(nr), sem(2), sem(nr),
        sem(nr), sem(nr), sem(2), sem(nr),
        sem(2), sem(2),
        sem(na), sem(na), sem(mh), sem(mh), sem(na), sem(na),
        sem(na), sem(na), sem(mh), sem(mh),
        sem(na), sem(na), sem(mh), sem(mh), sem(na), sem(na),
        sem(nr), sem(nr), sem(nr), sem(nr),
    ]
    space = pl.BlockSpec(memory_space=pltpu.VMEM)
    basis, triangle, interface = pl.pallas_call(
        functools.partial(kernel, nm, nr, ml, scale),
        out_shape=(
            jax.ShapeDtypeStruct((height, piece, width), F32),
            jax.ShapeDtypeStruct((width, width), F32),
            jax.ShapeDtypeStruct((3, piece, width), F32),
        ),
        in_specs=[pl.BlockSpec(memory_space=pltpu.HBM)] * 4 + [space],
        out_specs=(space,) * 3,
        scratch_shapes=scratch,
        compiler_params=pltpu.CompilerParams(
            collective_id=0, has_side_effects=True, vmem_limit_bytes=60 * 1024 * 1024
        ),
    )(
        start_core, right_side, left_interface,
        right_interface.reshape(3 * width, width), couplings,
    )
    return basis, triangle, interface


def solution(mesh):
    placed = (
        P("mode", "rank", None),
        P("mode", "rank", None),
        P(),
        P(),
        P(None, None, None, "mode"),
    )
    return jax.shard_map(
        functools.partial(shards, mesh.shape["mode"], mesh.shape["rank"]),
        mesh=mesh,
        in_specs=placed,
        out_specs=(P("mode", "rank", None), P(), P(None, "rank", None)),
        check_vma=False,
    )
```
